256 devices in a mesh: ctx: 32 (over z, x), exp: 8 (over y, core).
Axes of the slice: x: 4, y: 4, z: 8, core: 2. Of those that a mesh axis runs over, the one named last changes fastest.
Arguments:
- tokens: bfloat16 [24576, 6144], P('ctx', 'exp'), may hold values from -6 to 6
- keys: bfloat16 [24576, 1024], P('ctx', 'exp'), may hold values from -140 to 140
- values: bfloat16 [24576, 1024], P('ctx', 'exp'), may hold values from -6 to 6
- expert_ids: int32 [24576, 2], P('ctx'), may hold values from 0 to 7, all different within a row; in each aligned block of 768 rows (0 to 767, 768 to 1535, ...) at most 216 rows name the same one
- router_logits: float32 [24576, 2], P('ctx'), may hold values from -6 to 6
- query_weight: bfloat16 [8, 6144, 512], P('exp'), may hold values from -0.078125 to 0.078125
- output_weight: bfloat16 [8, 512, 6144], P('exp', None, 'ctx'), may hold values from -0.25 to 0.25
Outputs:
- mixed: bfloat16 [24576, 6144], P('ctx', 'exp')
The draws below stay inside these ranges and needn't reach their ends.
Inputs may be any that keep to these rules, and one draw needn't show every extreme that they name: `expert_ids`: each row names two different experts. Among the 768 rows of one block no expert is named more than 216 times, and in every draw some expert is named exactly 216 times in some block.
All inputs are finite; a program needn't handle non-finite values.
Results may differ from the reference program's by a relative error of at most 0.012.
The reference program's roundings to bfloat16 on the way count: a program that leaves them out, or rounds other values in their place, can miss the bound.
Values may be sent and summed in bfloat16 or wider, within the bound.
No kernel may reach another device: no remote copies, remote signals or barrier semaphores. Data moves between devices by JAX's collectives and lax.ppermute only.
A program may use at most 128 MiB of HBM per device.

```python
import math
import jax
import jax.numpy as jnp
import numpy as np
from jax import lax

D = 6144
QH = 4
HD = 128
KVH = 8
TOPK = 2
TOK_CTX = 768
EXPERTS = 8
SEQ = 24576
CAP = 216
N_CTX = 32


def draw_keys(key, part):
    key = jax.random.fold_in(key, 11)
    first = jax.random.fold_in(key, 0)
    base = jnp.clip(jax.random.normal(first, (SEQ, KVH * HD), jnp.float32), -4.0, 4.0)
    return base.astype(jnp.bfloat16)


def steps_of(own_key, dims, pieces, smallest, top_value):
    loudness = 1.0
    for dim, blocks in pieces:
        draws = jax.random.uniform(jax.random.fold_in(jax.random.fold_in(own_key, 6), dim), (blocks,), jnp.float32, smallest / len(pieces), top_value / len(pieces))
        loudness = loudness * jnp.repeat(jnp.exp(draws), dims[dim] // blocks).reshape((-1,) + (1,) * (len(dims) - 1 - dim))
    return loudness


def shared_out(key, own, number, rows, amount, top, reach, lean):
    sequence = jax.random.permutation(key, amount)
    packed, ordinary = shares(amount, rows * top, reach, lean, True), shares(amount, rows * top, reach, lean, False)
    places = jnp.arange(amount)

    def named(sizes, rotation):
        used = int((sizes > 0).sum())
        fixed = max(1, used // 4)
        shifted = fixed + (places - fixed + rotation * (used - fixed)) % max(1, amount - fixed)
        return jnp.zeros((amount,), jnp.int32).at[sequence[jnp.where(places < fixed, places, shifted)]].set(jnp.asarray(sizes, jnp.int32))

    sizes = jnp.where(number % 4 == 0, named(packed, number // 4), named(ordinary, number - number // 4 - 1))
    mixed = jax.random.permutation(jax.random.fold_in(own, 3), amount)
    donor, taker = mixed[0:amount // 2 * 2:2], mixed[1:amount // 2 * 2:2]
    slack = jnp.minimum(sizes[donor] - 1, reach - sizes[taker]) // 2
    slack = jnp.where((donor == sequence[0]) | (taker == sequence[0]) | (sizes[taker] == 0), 0, jnp.maximum(slack, 0))
    shifted = jax.random.randint(jax.random.fold_in(own, 4), (amount // 2,), 0, 1 << 20) % (slack + 1)
    sizes = sizes.at[donor].add(-shifted).at[taker].add(shifted)
    items = jnp.searchsorted(jnp.cumsum(sizes), jnp.arange(rows * top), side="right").astype(jnp.int32)
    table = items.reshape(top, rows).T
    table = table[jax.random.permutation(jax.random.fold_in(own, 1), rows)]
    rotation = jax.random.randint(jax.random.fold_in(own, 2), (rows, 1), 0, top)
    return jnp.take_along_axis(table, (jnp.arange(top)[None, :] + rotation) % top, axis=1)


def shares(amount, total, reach, lean, full):
    weights = [(1 << 20) // math.isqrt(grade ** lean) + 1 for grade in range(1, amount + 1)]
    largest = reach if full else min(reach, max(-(-total // amount), total * weights[0] // sum(weights)))
    least = 1 if total - largest >= amount - 1 else 0
    given, surplus = [largest] + [least] * (amount - 1), total - largest - least * (amount - 1)
    while surplus > 0:
        candidates = [i for i in range(1, amount) if given[i] < largest] or [i for i in range(1, amount) if given[i] < reach]
        pool, remaining = sum([weights[i] for i in candidates]), surplus
        for i in candidates:
            extra = min(reach - given[i], max(1, remaining * weights[i] // pool), surplus)
            given[i] = given[i] + extra
            surplus = surplus - extra
    return np.array(given)


def noise(key, shape, deviation, most, cuts=(), kind=jnp.bfloat16):
    drawn = deviation * jax.random.normal(key, shape, jnp.float32)
    if cuts:
        drawn = drawn * steps_of(key, shape, cuts, -0.22, 0.18)
    return jnp.clip(drawn, -most, most).astype(kind)


def setup_inputs(seed: int = 0) -> dict:
    arg_keys = jax.random.split(jax.random.key(seed), 8)
    tokens = noise(arg_keys[0], (SEQ, D), 1.0, 6.0, ((0, 32), (1, 8)))
    keys = draw_keys(jax.random.fold_in(arg_keys[7], 71), 0)
    values = noise(arg_keys[2], (SEQ, KVH * HD), 1.0, 6.0, ((0, 32), (1, 8)))
    expert_ids_keys = jax.random.split(jax.random.fold_in(arg_keys[3], 1), SEQ // TOK_CTX)
    expert_ids_turns = jax.random.permutation(jax.random.fold_in(arg_keys[3], 3), SEQ // TOK_CTX)
    expert_ids = jax.vmap(lambda own, number: shared_out(jax.random.fold_in(arg_keys[3], 2), own, number, TOK_CTX, EXPERTS, 2, CAP, 2))(expert_ids_keys, expert_ids_turns).reshape((SEQ, TOPK))
    router_logits = noise(arg_keys[4], (SEQ, TOPK), 1.5, 6.0, ((0, 32),), jnp.float32)
    query_weight = noise(arg_keys[5], (EXPERTS, D, QH * HD), D ** -0.5, 0.078125, ((0, 8),))
    output_weight = noise(arg_keys[6], (EXPERTS, QH * HD, D), (QH * HD) ** -0.5, 0.25, ((0, 8), (2, 32)))
    return {"tokens": tokens, "keys": keys, "values": values, "expert_ids": expert_ids, "router_logits": router_logits, "query_weight": query_weight, "output_weight": output_weight}


NEG = -1.0e30


def place_slots(expert_ids, count, capacity):
    tok = expert_ids.shape[0]
    flat = expert_ids.reshape(tok * 2).astype(jnp.int32)
    onehot = (flat[:, None] == jnp.arange(count, dtype=jnp.int32)[None, :]).astype(jnp.int32)
    before = jnp.cumsum(onehot, axis=0) - onehot
    slots = jnp.sum(before * onehot, axis=1).astype(jnp.int32)
    target = (flat * capacity + slots).astype(jnp.int32)
    owner = (jnp.arange(tok * 2, dtype=jnp.int32) // 2).astype(jnp.int32)
    table = jnp.full((count * capacity,), tok, jnp.int32).at[target].set(owner)
    return table, target.reshape(tok, 2)


def reference(tokens, keys, values, expert_ids, router_logits, query_weight, output_weight):
    stride = KVH // EXPERTS
    scale = HD ** -0.5
    blocks_x = tokens.reshape(N_CTX, TOK_CTX, D)
    blocks_ids = expert_ids.reshape(N_CTX, TOK_CTX, TOPK)
    blocks_gate = jax.nn.softmax(router_logits.astype(jnp.float32), axis=1).reshape(N_CTX, TOK_CTX, TOPK)
    key_pos = jnp.arange(SEQ, dtype=jnp.int32)

    def one_block(c):
        table, target = place_slots(blocks_ids[c], EXPERTS, CAP)
        padded = jnp.concatenate([blocks_x[c], jnp.zeros((1, D), tokens.dtype)], axis=0)

        def one_expert(e):
            rows = lax.dynamic_slice_in_dim(table, (e * CAP).astype(jnp.int32), CAP)
            chosen = jnp.take(padded, rows, axis=0)
            queries = jnp.dot(chosen, query_weight[e], preferred_element_type=jnp.float32).astype(jnp.bfloat16)
            qheads = queries.reshape(CAP, QH, HD).transpose(1, 0, 2)
            head = (e * stride * HD).astype(jnp.int32)
            khead = lax.dynamic_slice_in_dim(keys, head, HD, 1)
            vhead = lax.dynamic_slice_in_dim(values, head, HD, 1)
            positions = c * TOK_CTX + jnp.minimum(rows, TOK_CTX - 1)
            scores = jnp.einsum("hrd,kd->hrk", qheads.astype(jnp.float32), khead.astype(jnp.float32)) * scale
            allowed = key_pos[None, None, :] <= positions[None, :, None]
            scores = jnp.where(allowed, scores, NEG)
            top = jnp.max(scores, axis=2)
            weight = jnp.where(allowed, jnp.exp(scores - top[..., None]), 0.0)
            total = jnp.sum(weight, axis=2)
            probability = weight.astype(jnp.bfloat16)
            summed = jnp.einsum("hrk,kd->hrd", probability.astype(jnp.float32), vhead.astype(jnp.float32))
            attended = (summed / total[..., None]).transpose(1, 0, 2).reshape(CAP, QH * HD).astype(jnp.bfloat16)
            return jnp.dot(attended, output_weight[e], preferred_element_type=jnp.float32).astype(jnp.bfloat16)

        projected = lax.map(one_expert, jnp.arange(EXPERTS, dtype=jnp.int32))
        flat = projected.reshape(EXPERTS * CAP, D)
        picked = jnp.take(flat, target.reshape(-1), axis=0).reshape(TOK_CTX, TOPK, D)
        mixed = jnp.sum(blocks_gate[c][..., None] * picked.astype(jnp.float32), axis=1)
        return mixed.astype(jnp.bfloat16)

    out = lax.map(one_block, jnp.arange(N_CTX, dtype=jnp.int32))
    return out.reshape(SEQ, D)
```

```python
import jax
import jax.numpy as jnp
from jax import lax
from jax.experimental import pallas as pl
from jax.experimental.pallas import tpu as pltpu
from jax.sharding import Mesh, PartitionSpec as P

QH = 4
HD = 128
Z, X, Y, CORE = 8, 4, 4, 2
EXPERTS = 8
TOK = 768
CAP = 216
STAT = 224
WIDE = 768
THIRDS = 3
THIRD = WIDE // THIRDS
COLS = 192
NEG = -1e30
SCALE2 = HD ** (-0.5) * 1.4426950408889634
F32 = jnp.float32
BF16 = jnp.bfloat16
CTX = ("z", "x")
EXP = ("y", "core")


def params(mebibytes=60):
    return pltpu.CompilerParams(vmem_limit_bytes=mebibytes * 1024 * 1024)


def whole(shape):
    return pl.BlockSpec(shape, lambda *_: (0,) * len(shape))


def nt(a, b):
    return lax.dot_general(a, b, (((1,), (1,)), ((), ())), preferred_element_type=F32)


def dispatch_kernel(
    me_ref, ids_ref, tok_hbm, key_hbm, value_hbm, *refs
):
    out_hbms = refs[:THIRDS]
    own_hbm, pos_ref, tok_ref, row_ref, sems, out_sems = refs[THIRDS:]
    load = pltpu.make_async_copy(tok_hbm, tok_ref, sems.at[0])
    load.start()
    sides = [
        pltpu.make_async_copy(key_hbm, own_hbm.at[:, :HD], sems.at[1]),
        pltpu.make_async_copy(value_hbm, own_hbm.at[:, HD:], sems.at[2]),
    ]
    for side in sides:
        side.start()
    row = lax.broadcasted_iota(jnp.int32, (EXPERTS, TOK), 0)
    member = (ids_ref[0:1, :] == row) | (ids_ref[1:2, :] == row)
    before = lax.broadcasted_iota(jnp.int32, (TOK, TOK), 0) < lax.broadcasted_iota(
        jnp.int32, (TOK, TOK), 1
    )
    slots = jnp.dot(
        jnp.where(member, 1.0, 0.0).astype(BF16),
        jnp.where(before, 1.0, 0.0).astype(BF16),
        preferred_element_type=F32,
    )
    slots = jnp.where(member, slots, -1.0).astype(jnp.int32)
    load.wait()
    place = lax.broadcasted_iota(jnp.int32, (CAP, TOK), 1).astype(F32)
    sends = []
    for e in range(EXPERTS):
        hit = lax.broadcasted_iota(jnp.int32, (CAP, TOK), 0) == slots[e : e + 1, :]
        row_ref[e] = jnp.dot(
            jnp.where(hit, 1.0, 0.0).astype(BF16), tok_ref[...], preferred_element_type=F32
        ).astype(BF16)
        for c in range(THIRDS):
            send = pltpu.make_async_copy(
                row_ref.at[e, :, pl.ds(c * THIRD, THIRD)], out_hbms[c].at[e], out_sems.at[c, e]
            )
            send.start()
            sends.append(send)

        @pl.when(e == me_ref[0])
        def _():
            pos = jnp.max(jnp.where(hit, place, -1.0), axis=1, keepdims=True)
            pos = jnp.where(pos < 0.0, float(TOK - 1), pos)
            pos_ref[...] = jnp.broadcast_to(pos, (CAP, HD))

    for copy in sends + sides:
        copy.wait()


def dispatch(me, ids_t, tokens, keys, values):
    anywhere = pl.BlockSpec(memory_space=pltpu.HBM)
    return pl.pallas_call(
        dispatch_kernel,
        in_specs=[
            pl.BlockSpec(memory_space=pltpu.SMEM),
            pl.BlockSpec(memory_space=pltpu.VMEM),
            anywhere,
            anywhere,
            anywhere,
        ],
        out_specs=[anywhere] * (THIRDS + 1) + [pl.BlockSpec(memory_space=pltpu.VMEM)],
        out_shape=[jax.ShapeDtypeStruct((EXPERTS, CAP, THIRD), BF16)] * THIRDS
        + [
            jax.ShapeDtypeStruct((TOK, 2 * HD), BF16),
            jax.ShapeDtypeStruct((CAP, HD), F32),
        ],
        scratch_shapes=[
            pltpu.VMEM((TOK, WIDE), BF16),
            pltpu.VMEM((EXPERTS, CAP, WIDE), BF16),
            pltpu.SemaphoreType.DMA((3,)),
            pltpu.SemaphoreType.DMA((THIRDS, EXPERTS)),
        ],
        cost_estimate=pl.CostEstimate(
            flops=2 * EXPERTS * CAP * TOK * WIDE,
            bytes_accessed=(EXPERTS * CAP + TOK) * WIDE * 2,
            transcendentals=0,
        ),
        compiler_params=params(),
        name="dispatch",
    )(me, ids_t, tokens, keys, values)


def query_kernel(*refs):
    x_hbms, (w_hbm, q_ref, x_ref, w_ref, sems) = refs[:THIRDS], refs[THIRDS:]
    loads = []
    for j in range(EXPERTS):
        group = [
            pltpu.make_async_copy(
                w_hbm.at[0, pl.ds(j * WIDE, WIDE), :], w_ref.at[j], sems.at[THIRDS, j]
            )
        ]
        for c in range(THIRDS):
            group.append(
                pltpu.make_async_copy(
                    x_hbms[c].at[j], x_ref.at[j, :, pl.ds(c * THIRD, THIRD)], sems.at[c, j]
                )
            )
        for load in group:
            load.start()
        loads.append(group)
    total = None
    for j, group in enumerate(loads):
        for load in group:
            load.wait()
        part = jnp.dot(x_ref[j], w_ref[j], preferred_element_type=F32)
        total = part if total is None else total + part
    for h in range(QH):
        q_ref[h] = total[:, h * HD : (h + 1) * HD].astype(BF16)


def project_queries(rows, weight):
    return pl.pallas_call(
        query_kernel,
        in_specs=[pl.BlockSpec(memory_space=pltpu.HBM)] * (THIRDS + 1),
        out_specs=pl.BlockSpec(memory_space=pltpu.VMEM),
        out_shape=jax.ShapeDtypeStruct((QH, CAP, HD), BF16),
        scratch_shapes=[
            pltpu.VMEM((EXPERTS, CAP, WIDE), BF16),
            pltpu.VMEM((EXPERTS, WIDE, QH * HD), BF16),
            pltpu.SemaphoreType.DMA((THIRDS + 1, EXPERTS)),
        ],
        cost_estimate=pl.CostEstimate(
            flops=2 * EXPERTS * CAP * WIDE * QH * HD,
            bytes_accessed=EXPERTS * WIDE * (CAP + QH * HD) * 2,
            transcendentals=0,
        ),
        compiler_params=params(),
        name="queries",
    )(*rows, weight)


def attend_kernel(masked, use_ref, q_ref, pos_ref, *refs):
    kv_hbms = refs[:8]
    out_ref, kv_ref, top_ref, acc_ref, sems = refs[8:]
    wanted = [(lambda f: f()) if masked and i == 0 else pl.when(use_ref[i] > 0) for i in range(8)]
    loads = [pltpu.make_async_copy(kv_hbms[i], kv_ref.at[i], sems.at[i]) for i in range(8)]
    for i in range(8):
        wanted[i](lambda i=i: loads[i].start())
    top_ref[...] = jnp.full(top_ref.shape, NEG, F32)
    acc_ref[...] = jnp.zeros(acc_ref.shape, F32)

    def block(i):
        mask = masked and i == 0
        loads[i].wait()
        k = kv_ref[i, :, :HD]
        v = jnp.concatenate([kv_ref[i, :, HD:], jnp.ones((TOK, HD), BF16)], axis=1)
        scores = [nt(q_ref[h], k) for h in range(QH)]
        for h in range(QH):
            s = scores[h]
            if mask:
                place = lax.broadcasted_iota(jnp.int32, (CAP, TOK), 1).astype(F32)
                s = jnp.where(place <= pos_ref[:, 0:1], s, NEG)
            old = top_ref[h]
            new = jnp.maximum(old, jnp.max(s, axis=1, keepdims=True))
            p = jnp.exp2((s - jnp.concatenate([new] * (TOK // 128), axis=1)) * SCALE2)
            shrink = jnp.exp2((old - new) * SCALE2)
            acc_ref[h] = acc_ref[h] * jnp.concatenate([shrink, shrink], axis=1) + jnp.dot(
                p.astype(BF16), v, preferred_element_type=F32
            )
            top_ref[h] = new

    for i in range(8):
        wanted[i](lambda i=i: block(i))

    for h in range(QH):
        total = acc_ref[h, :, HD:]
        some = total > 0.0
        safe = jnp.where(some, total, 1.0)
        out_ref[h, :CAP, :] = (acc_ref[h, :, :HD] / safe).astype(BF16)
        out_ref[h, CAP:STAT, :] = jnp.zeros((STAT - CAP, HD), BF16)
        stat = jnp.where(some, top_ref[h] * SCALE2 + jnp.log2(safe), NEG)
        stat = jnp.concatenate([stat, jnp.zeros((256 - CAP, HD), F32)], axis=0).T[0:16, :]
        line = lax.broadcasted_iota(jnp.int32, (16, HD), 0)
        spread = jnp.where(lax.rem(line, 2) == 0, stat[:, :HD], stat[:, HD:])
        high = spread.astype(BF16).astype(F32)
        middle = (spread - high).astype(BF16).astype(F32)
        low = spread - high - middle
        parts = jnp.where(line < 2, high, jnp.where(line < 4, middle, low))
        out_ref[h, STAT:, :] = parts.astype(BF16)


def attend(masked, use, q, pos, blocks):
    name = "attend_own" if masked else "attend_near"
    return pl.pallas_call(
        lambda *refs: attend_kernel(masked, *refs),
        in_specs=[pl.BlockSpec(memory_space=pltpu.SMEM)]
        + [pl.BlockSpec(memory_space=pltpu.VMEM)] * 2
        + [pl.BlockSpec(memory_space=pl.ANY)] * len(blocks),
        out_specs=pl.BlockSpec(memory_space=pltpu.VMEM),
        out_shape=jax.ShapeDtypeStruct((QH, STAT + 16, HD), BF16),
        scratch_shapes=[
            pltpu.VMEM((len(blocks), TOK, 2 * HD), BF16),
            pltpu.VMEM((QH, CAP, HD), F32),
            pltpu.VMEM((QH, CAP, 2 * HD), F32),
            pltpu.SemaphoreType.DMA((len(blocks),)),
        ],
        cost_estimate=pl.CostEstimate(
            flops=4 * QH * CAP * HD * 4 * TOK,
            bytes_accessed=8 * TOK * 2 * HD * 2,
            transcendentals=QH * CAP * 4 * TOK,
        ),
        compiler_params=params(),
        name=name,
    )(use, q, pos, *blocks)


def combine_kernel(*refs):
    outs, out_ref = refs[:4], refs[4]
    for h in range(QH):
        logs = []
        for o in outs:
            parts = o[h, STAT:, :].astype(F32)
            even = parts[0:1] + parts[2:3] + parts[4:5]
            odd = parts[1:2] + parts[3:4] + parts[5:6]
            stat = jnp.concatenate([even, odd], axis=1)
            logs.append(jnp.broadcast_to(stat, (HD, 256)).T[:CAP, :])
        top = jnp.maximum(jnp.maximum(logs[0], logs[1]), jnp.maximum(logs[2], logs[3]))
        weights = [jnp.exp2(v - top) for v in logs]
        total = weights[0] + weights[1] + weights[2] + weights[3]
        summed = sum(w * o[h, :CAP, :].astype(F32) for w, o in zip(weights, outs))
        out_ref[:, h * HD : (h + 1) * HD] = (summed / total).astype(BF16)


def combine(outs):
    return pl.pallas_call(
        combine_kernel,
        out_shape=jax.ShapeDtypeStruct((CAP, QH * HD), BF16),
        compiler_params=params(),
        name="combine",
    )(*outs)


def output_kernel(
    order_ref, mine_ref, other_ref, w_hbm, ids_ref, logit_ref, out_ref, w_ref, acc_ref, sems
):
    loads = [
        pltpu.make_async_copy(w_hbm.at[order_ref[j]], w_ref.at[j], sems.at[j])
        for j in range(EXPERTS)
    ]
    for load in loads:
        load.start()
    lane = lax.broadcasted_iota(jnp.int32, (TOK, HD), 1)
    first = ids_ref[:, 0:1] == lane
    second = ids_ref[:, 1:2] == lane
    member = first | second
    before = lax.broadcasted_iota(jnp.int32, (TOK, TOK), 1) < lax.broadcasted_iota(
        jnp.int32, (TOK, TOK), 0
    )
    slots = jnp.dot(
        jnp.where(before, 1.0, 0.0).astype(BF16),
        jnp.where(member, 1.0, 0.0).astype(BF16),
        preferred_element_type=F32,
    )
    slots = jnp.where(member, slots, -1.0)
    l0, l1 = logit_ref[:, 0:1], logit_ref[:, 1:2]
    top = jnp.maximum(l0, l1)
    w0, w1 = jnp.exp(l0 - top), jnp.exp(l1 - top)
    total = w0 + w1
    gates = jnp.where(first, w0 / total, jnp.where(second, w1 / total, 0.0))
    for j in range(EXPERTS):
        rows = (mine_ref if j % 2 == 0 else other_ref)[j // 2]
        here = lane == order_ref[j]
        slot = jnp.sum(jnp.where(here, slots, 0.0), axis=1, keepdims=True).astype(jnp.int32)
        gate = jnp.sum(jnp.where(here, gates, 0.0), axis=1, keepdims=True)
        hit = lax.broadcasted_iota(jnp.int32, (TOK, CAP), 1) == slot
        spread = jnp.where(hit, gate, 0.0).astype(BF16)
        loads[j].wait()
        projected = nt(rows, w_ref[j]).astype(BF16)
        part = jnp.dot(spread, projected, preferred_element_type=F32)
        if j == 0:
            acc_ref[...] = part
        elif j < EXPERTS - 1:
            acc_ref[...] += part
        else:
            out_ref[...] = (acc_ref[...] + part).astype(BF16)


def project_output(order, mine, other, weight, ids, logits):
    vmem = pl.BlockSpec(memory_space=pltpu.VMEM)
    return pl.pallas_call(
        output_kernel,
        in_specs=[
            pl.BlockSpec(memory_space=pltpu.SMEM),
            vmem,
            vmem,
            pl.BlockSpec(memory_space=pltpu.HBM),
            vmem,
            vmem,
        ],
        out_specs=vmem,
        out_shape=jax.ShapeDtypeStruct((TOK, WIDE), BF16),
        scratch_shapes=[
            pltpu.VMEM((EXPERTS, WIDE, QH * HD), BF16),
            pltpu.VMEM((TOK, WIDE), F32),
            pltpu.SemaphoreType.DMA((EXPERTS,)),
        ],
        cost_estimate=pl.CostEstimate(
            flops=2 * EXPERTS * CAP * WIDE * (QH * HD + TOK),
            bytes_accessed=EXPERTS * WIDE * QH * HD * 2,
            transcendentals=0,
        ),
        compiler_params=params(),
        name="output",
    )(order, mine, other, weight, ids, logits)


def turn(n, by):
    return [(i, (i + by) % n) for i in range(n)]


def local(tokens, keys, values, expert_ids, router_logits, query_weight, output_weight):
    z = lax.axis_index("z")
    x = lax.axis_index("x")
    y = lax.axis_index("y")
    core = lax.axis_index("core")
    me = y * CORE + core

    piece = output_weight[0].T
    moves = [
        ((ep * X + i) * EXPERTS + e, (e * X + i) * EXPERTS + ep)
        for ep in range(Z)
        for e in range(EXPERTS)
        for i in range(X)
    ]
    piece = lax.ppermute(piece, CTX + EXP, moves)

    *outgoing, own, pos = dispatch(me[None], expert_ids.T, tokens, keys, values)
    incoming = [
        lax.all_to_all(part, EXP, split_axis=0, concat_axis=0, tiled=True) for part in outgoing
    ]

    up, down = [], []
    above = below = own
    for s in range(1, 5):
        if s > 1:
            above, below, incoming[s - 2] = lax.optimization_barrier(
                (above, below, incoming[s - 2])
            )
        above = lax.ppermute(above, "z", [(i - 1, i) for i in range(s, Z)])
        if s < 4:
            below = lax.ppermute(
                below, "z", [((i + 1) % Z, i % Z) for i in range(Z - s, Z - s + 3)]
            )
            down.append(below)
        up.append(above)
    blocks = [own] + up + down
    used = [z >= s for s in range(1, 5)] + [z >= Z - s for s in range(1, 4)]

    piece, _ = lax.optimization_barrier((piece, incoming[0]))
    columns = lax.all_gather(piece, CTX, axis=0, tiled=True).reshape(EXPERTS, WIDE, QH * HD)
    q = project_queries(incoming, query_weight)

    shifts = (2, 1, 3)
    theirs = [lax.ppermute(q, "x", turn(X, s)) for s in shifts]

    def flags(first):
        return jnp.stack([first] + used).astype(jnp.int32)

    outs = [attend(True, flags(z >= 0), q, pos, blocks)]
    theirs, _ = lax.optimization_barrier((theirs, outs[0]))
    for s, other in zip(shifts, theirs):
        source = lax.rem(x + (X - s), X)
        o = attend(False, flags(x < source), other, pos, blocks)
        outs.append(lax.ppermute(o, "x", turn(X, X - s)))
    attended = combine(outs)

    near = [lax.ppermute(attended, "y", turn(Y, s)) for s in range(1, Y)]
    mine = jnp.stack([attended] + near)
    other = lax.ppermute(mine, "core", [(0, 1), (1, 0)])
    order = jnp.stack(
        [
            lax.rem(y + (Y - s), Y) * CORE + (core if same else 1 - core)
            for s in range(Y)
            for same in (True, False)
        ]
    ).astype(jnp.int32)
    return project_output(order, mine, other, columns, expert_ids, router_logits)


def solution(mesh):
    fine = Mesh(mesh.devices.reshape(Z, X, Y, CORE), ("z", "x", "y", "core"))
    return jax.shard_map(
        local,
        mesh=fine,
        in_specs=(
            P(CTX, EXP),
            P(CTX, EXP),
            P(CTX, EXP),
            P(CTX, None),
            P(CTX, None),
            P(EXP, None, None),
            P(EXP, None, CTX),
        ),
        out_specs=P(CTX, EXP),
        check_vma=False,
    )
```

```python
import jax
import jax.numpy as jnp
from jax import lax
from jax.experimental import pallas as pl
from jax.experimental.pallas import tpu as pltpu
from jax.sharding import Mesh, PartitionSpec as P

QH = 4
HD = 128
Z, X, Y, CORE = 8, 4, 4, 2
EXPERTS = 8
TOK = 768
CAP = 216
STAT = 224
WIDE = 768
COLS = 192
NEG = -1e30
SCALE2 = HD ** (-0.5) * 1.4426950408889634
F32 = jnp.float32
BF16 = jnp.bfloat16
CTX = ("z", "x")
EXP = ("y", "core")


def params(mebibytes=16):
    return pltpu.CompilerParams(vmem_limit_bytes=mebibytes * 1024 * 1024)


def whole(shape):
    return pl.BlockSpec(shape, lambda *_: (0,) * len(shape))


def nt(a, b):
    return lax.dot_general(a, b, (((1,), (1,)), ((), ())), preferred_element_type=F32)


def join_kernel(key_ref, value_ref, out_ref):
    out_ref[:, :HD] = key_ref[...]
    out_ref[:, HD:] = value_ref[...]


def join(keys, values):
    return pl.pallas_call(
        join_kernel,
        out_shape=jax.ShapeDtypeStruct((TOK, 2 * HD), BF16),
        compiler_params=params(60),
        name="join",
    )(keys, values)


def dispatch_kernel(
    me_ref, ids_ref, tok_hbm, out_hbm, pos_ref, tok_ref, row_ref, load_sem, out_sems
):
    load = pltpu.make_async_copy(tok_hbm, tok_ref, load_sem)
    load.start()
    row = lax.broadcasted_iota(jnp.int32, (EXPERTS, TOK), 0)
    member = (ids_ref[0:1, :] == row) | (ids_ref[1:2, :] == row)
    before = lax.broadcasted_iota(jnp.int32, (TOK, TOK), 0) < lax.broadcasted_iota(
        jnp.int32, (TOK, TOK), 1
    )
    slots = jnp.dot(
        jnp.where(member, 1.0, 0.0).astype(BF16),
        jnp.where(before, 1.0, 0.0).astype(BF16),
        preferred_element_type=F32,
    )
    slots = jnp.where(member, slots, -1.0).astype(jnp.int32)
    load.wait()
    place = lax.broadcasted_iota(jnp.int32, (CAP, TOK), 1).astype(F32)
    sends = []
    for e in range(EXPERTS):
        hit = lax.broadcasted_iota(jnp.int32, (CAP, TOK), 0) == slots[e : e + 1, :]
        row_ref[e] = jnp.dot(
            jnp.where(hit, 1.0, 0.0).astype(BF16), tok_ref[...], preferred_element_type=F32
        ).astype(BF16)
        send = pltpu.make_async_copy(row_ref.at[e], out_hbm.at[e], out_sems.at[e])
        send.start()
        sends.append(send)

        @pl.when(e == me_ref[0])
        def _():
            pos = jnp.max(jnp.where(hit, place, -1.0), axis=1, keepdims=True)
            pos = jnp.where(pos < 0.0, float(TOK - 1), pos)
            pos_ref[...] = jnp.broadcast_to(pos, (CAP, HD))

    for send in sends:
        send.wait()


def dispatch(me, ids_t, tokens):
    return pl.pallas_call(
        dispatch_kernel,
        in_specs=[
            pl.BlockSpec(memory_space=pltpu.SMEM),
            pl.BlockSpec(memory_space=pltpu.VMEM),
            pl.BlockSpec(memory_space=pltpu.HBM),
        ],
        out_specs=[
            pl.BlockSpec(memory_space=pltpu.HBM),
            pl.BlockSpec(memory_space=pltpu.VMEM),
        ],
        out_shape=[
            jax.ShapeDtypeStruct((EXPERTS, CAP, WIDE), BF16),
            jax.ShapeDtypeStruct((CAP, HD), F32),
        ],
        scratch_shapes=[
            pltpu.VMEM((TOK, WIDE), BF16),
            pltpu.VMEM((EXPERTS, CAP, WIDE), BF16),
            pltpu.SemaphoreType.DMA,
            pltpu.SemaphoreType.DMA((EXPERTS,)),
        ],
        cost_estimate=pl.CostEstimate(
            flops=2 * EXPERTS * CAP * TOK * WIDE,
            bytes_accessed=(EXPERTS * CAP + TOK) * WIDE * 2,
            transcendentals=0,
        ),
        compiler_params=params(60),
        name="dispatch",
    )(me, ids_t, tokens)


def query_kernel(x_hbm, w_hbm, q_ref, x_ref, w_ref, sems):
    loads = []
    for j in range(EXPERTS):
        rows = pltpu.make_async_copy(x_hbm.at[j], x_ref.at[j], sems.at[0, j])
        weight = pltpu.make_async_copy(
            w_hbm.at[0, pl.ds(j * WIDE, WIDE), :], w_ref.at[j], sems.at[1, j]
        )
        rows.start()
        weight.start()
        loads.append((rows, weight))
    total = None
    for j, (rows, weight) in enumerate(loads):
        rows.wait()
        weight.wait()
        part = jnp.dot(x_ref[j], w_ref[j], preferred_element_type=F32)
        total = part if total is None else total + part
    for h in range(QH):
        q_ref[h] = total[:, h * HD : (h + 1) * HD].astype(BF16)


def project_queries(rows, weight):
    return pl.pallas_call(
        query_kernel,
        in_specs=[pl.BlockSpec(memory_space=pltpu.HBM)] * 2,
        out_specs=pl.BlockSpec(memory_space=pltpu.VMEM),
        out_shape=jax.ShapeDtypeStruct((QH, CAP, HD), BF16),
        scratch_shapes=[
            pltpu.VMEM((EXPERTS, CAP, WIDE), BF16),
            pltpu.VMEM((EXPERTS, WIDE, QH * HD), BF16),
            pltpu.SemaphoreType.DMA((2, EXPERTS)),
        ],
        cost_estimate=pl.CostEstimate(
            flops=2 * EXPERTS * CAP * WIDE * QH * HD,
            bytes_accessed=EXPERTS * WIDE * (CAP + QH * HD) * 2,
            transcendentals=0,
        ),
        compiler_params=params(60),
        name="queries",
    )(rows, weight)


def attend_kernel(masked, place_ref, own_ref, q_ref, pos_ref, kv_hbm, out_ref, kv_ref, top_ref, acc_ref, sems):
    z = place_ref[0]

    def wanted(i):
        return pl.when(i < z) if i < Z - 1 else pl.when(own_ref[0] > 0)

    loads = [
        pltpu.make_async_copy(kv_hbm.at[i if i < Z - 1 else z], kv_ref.at[i], sems.at[i])
        for i in range(Z)
    ]
    for i in range(Z):
        wanted(i)(lambda i=i: loads[i].start())
    top_ref[...] = jnp.full(top_ref.shape, NEG, F32)
    acc_ref[...] = jnp.zeros(acc_ref.shape, F32)

    def block(i):
        mask = masked and i == Z - 1
        loads[i].wait()
        k = kv_ref[i, :, :HD]
        v = jnp.concatenate([kv_ref[i, :, HD:], jnp.ones((TOK, HD), BF16)], axis=1)
        scores = [nt(q_ref[h], k) for h in range(QH)]
        for h in range(QH):
            s = scores[h]
            if mask:
                place = lax.broadcasted_iota(jnp.int32, (CAP, TOK), 1).astype(F32)
                s = jnp.where(place <= pos_ref[:, 0:1], s, NEG)
            old = top_ref[h]
            new = jnp.maximum(old, jnp.max(s, axis=1, keepdims=True))
            p = jnp.exp2((s - jnp.concatenate([new] * (TOK // 128), axis=1)) * SCALE2)
            shrink = jnp.exp2((old - new) * SCALE2)
            acc_ref[h] = acc_ref[h] * jnp.concatenate([shrink, shrink], axis=1) + jnp.dot(
                p.astype(BF16), v, preferred_element_type=F32
            )
            top_ref[h] = new

    for i in range(Z):
        wanted(i)(lambda i=i: block(i))

    for h in range(QH):
        total = acc_ref[h, :, HD:]
        some = total > 0.0
        safe = jnp.where(some, total, 1.0)
        out_ref[h, :CAP, :] = (acc_ref[h, :, :HD] / safe).astype(BF16)
        out_ref[h, CAP:STAT, :] = jnp.zeros((STAT - CAP, HD), BF16)
        stat = jnp.where(some, top_ref[h] * SCALE2 + jnp.log2(safe), NEG)
        stat = jnp.concatenate([stat, jnp.zeros((256 - CAP, HD), F32)], axis=0).T[0:16, :]
        line = lax.broadcasted_iota(jnp.int32, (16, HD), 0)
        spread = jnp.where(lax.rem(line, 2) == 0, stat[:, :HD], stat[:, HD:])
        high = spread.astype(BF16).astype(F32)
        middle = (spread - high).astype(BF16).astype(F32)
        low = spread - high - middle
        parts = jnp.where(line < 2, high, jnp.where(line < 4, middle, low))
        out_ref[h, STAT:, :] = parts.astype(BF16)


def attend(masked, place, own, q, pos, blocks):
    name = "attend_own" if masked else "attend_near"
    return pl.pallas_call(
        lambda *refs: attend_kernel(masked, *refs),
        in_specs=[pl.BlockSpec(memory_space=pltpu.SMEM)] * 2
        + [pl.BlockSpec(memory_space=pltpu.VMEM)] * 2
        + [pl.BlockSpec(memory_space=pl.ANY)],
        out_specs=pl.BlockSpec(memory_space=pltpu.VMEM),
        out_shape=jax.ShapeDtypeStruct((QH, STAT + 16, HD), BF16),
        scratch_shapes=[
            pltpu.VMEM((Z, TOK, 2 * HD), BF16),
            pltpu.VMEM((QH, CAP, HD), F32),
            pltpu.VMEM((QH, CAP, 2 * HD), F32),
            pltpu.SemaphoreType.DMA((Z,)),
        ],
        cost_estimate=pl.CostEstimate(
            flops=4 * QH * CAP * HD * 4 * TOK,
            bytes_accessed=8 * TOK * 2 * HD * 2,
            transcendentals=QH * CAP * 4 * TOK,
        ),
        compiler_params=params(),
        name=name,
    )(place, own, q, pos, blocks)


def combine_kernel(*refs):
    outs, out_ref = refs[:4], refs[4]
    for h in range(QH):
        logs = []
        for o in outs:
            parts = o[h, STAT:, :].astype(F32)
            even = parts[0:1] + parts[2:3] + parts[4:5]
            odd = parts[1:2] + parts[3:4] + parts[5:6]
            stat = jnp.concatenate([even, odd], axis=1)
            logs.append(jnp.broadcast_to(stat, (HD, 256)).T[:CAP, :])
        top = jnp.maximum(jnp.maximum(logs[0], logs[1]), jnp.maximum(logs[2], logs[3]))
        weights = [jnp.exp2(v - top) for v in logs]
        total = weights[0] + weights[1] + weights[2] + weights[3]
        summed = sum(w * o[h, :CAP, :].astype(F32) for w, o in zip(weights, outs))
        out_ref[:, h * HD : (h + 1) * HD] = (summed / total).astype(BF16)


def combine(outs):
    return pl.pallas_call(
        combine_kernel,
        out_shape=jax.ShapeDtypeStruct((CAP, QH * HD), BF16),
        compiler_params=params(),
        name="combine",
    )(*outs)


def output_kernel(
    order_ref, side_ref, mine_ref, other_ref, w_hbm, ids_ref, logit_ref, out_ref, w_ref, acc_ref, sems
):
    loads = [
        [
            pltpu.make_async_copy(
                w_hbm.at[order_ref[j], i],
                w_ref.at[j, pl.ds(pl.multiple_of(side_ref[i] * COLS, COLS), COLS), :],
                sems.at[j, i],
            )
            for i in range(X)
        ]
        for j in range(EXPERTS)
    ]
    for group in loads:
        for load in group:
            load.start()
    lane = lax.broadcasted_iota(jnp.int32, (TOK, HD), 1)
    first = ids_ref[:, 0:1] == lane
    second = ids_ref[:, 1:2] == lane
    member = first | second
    before = lax.broadcasted_iota(jnp.int32, (TOK, TOK), 1) < lax.broadcasted_iota(
        jnp.int32, (TOK, TOK), 0
    )
    slots = jnp.dot(
        jnp.where(before, 1.0, 0.0).astype(BF16),
        jnp.where(member, 1.0, 0.0).astype(BF16),
        preferred_element_type=F32,
    )
    slots = jnp.where(member, slots, -1.0)
    l0, l1 = logit_ref[:, 0:1], logit_ref[:, 1:2]
    top = jnp.maximum(l0, l1)
    w0, w1 = jnp.exp(l0 - top), jnp.exp(l1 - top)
    total = w0 + w1
    gates = jnp.where(first, w0 / total, jnp.where(second, w1 / total, 0.0))
    for j in range(EXPERTS):
        rows = (mine_ref if j % 2 == 0 else other_ref)[j // 2]
        here = lane == order_ref[j]
        slot = jnp.sum(jnp.where(here, slots, 0.0), axis=1, keepdims=True).astype(jnp.int32)
        gate = jnp.sum(jnp.where(here, gates, 0.0), axis=1, keepdims=True)
        hit = lax.broadcasted_iota(jnp.int32, (TOK, CAP), 1) == slot
        spread = jnp.where(hit, gate, 0.0).astype(BF16)
        for load in loads[j]:
            load.wait()
        projected = nt(rows, w_ref[j]).astype(BF16)
        part = jnp.dot(spread, projected, preferred_element_type=F32)
        if j == 0:
            acc_ref[...] = part
        elif j < EXPERTS - 1:
            acc_ref[...] += part
        else:
            out_ref[...] = (acc_ref[...] + part).astype(BF16)


def project_output(order, side, mine, other, weight, ids, logits):
    vmem = pl.BlockSpec(memory_space=pltpu.VMEM)
    return pl.pallas_call(
        output_kernel,
        in_specs=[
            pl.BlockSpec(memory_space=pltpu.SMEM),
            pl.BlockSpec(memory_space=pltpu.SMEM),
            vmem,
            vmem,
            pl.BlockSpec(memory_space=pltpu.HBM),
            vmem,
            vmem,
        ],
        out_specs=vmem,
        out_shape=jax.ShapeDtypeStruct((TOK, WIDE), BF16),
        scratch_shapes=[
            pltpu.VMEM((EXPERTS, WIDE, QH * HD), BF16),
            pltpu.VMEM((TOK, WIDE), F32),
            pltpu.SemaphoreType.DMA((EXPERTS, X)),
        ],
        cost_estimate=pl.CostEstimate(
            flops=2 * EXPERTS * CAP * WIDE * (QH * HD + TOK),
            bytes_accessed=EXPERTS * WIDE * QH * HD * 2,
            transcendentals=0,
        ),
        compiler_params=params(60),
        name="output",
    )(order, side, mine, other, weight, ids, logits)


def turn(n, by):
    return [(i, (i + by) % n) for i in range(n)]


def local(tokens, keys, values, expert_ids, router_logits, query_weight, output_weight):
    z = lax.axis_index("z")
    x = lax.axis_index("x")
    y = lax.axis_index("y")
    core = lax.axis_index("core")
    me = y * CORE + core

    blocks = lax.all_gather(join(keys, values), "z", axis=0)

    shifts = (2, 1, 3)
    piece = output_weight[0].T
    moves = [
        ((ep * X + i) * EXPERTS + e, (e * X + i) * EXPERTS + ep)
        for ep in range(Z)
        for e in range(EXPERTS)
        for i in range(X)
    ]
    piece = lax.ppermute(piece, CTX + EXP, moves)
    pieces = [piece] + [lax.ppermute(piece, "x", turn(X, s)) for s in shifts]

    outgoing, pos = dispatch(me[None], expert_ids.T, tokens)
    incoming = lax.all_to_all(outgoing, EXP, split_axis=0, concat_axis=0, tiled=True)
    pieces, _ = lax.optimization_barrier((jnp.stack(pieces), incoming))
    columns = lax.all_gather(pieces, "z", axis=0)
    q = project_queries(incoming, query_weight)

    theirs = [lax.ppermute(q, "x", turn(X, s)) for s in shifts]
    place = z[None].astype(jnp.int32)
    outs = [attend(True, place, jnp.ones((1,), jnp.int32), q, pos, blocks)]
    theirs, _ = lax.optimization_barrier((theirs, outs[0]))
    for s, other in zip(shifts, theirs):
        source = lax.rem(x + (X - s), X)
        o = attend(False, place, (x < source)[None].astype(jnp.int32), other, pos, blocks)
        outs.append(lax.ppermute(o, "x", turn(X, X - s)))
    attended = combine(outs)

    near = [lax.ppermute(attended, "y", turn(Y, s)) for s in range(1, Y)]
    mine = jnp.stack([attended] + near)
    other = lax.ppermute(mine, "core", [(0, 1), (1, 0)])
    order = jnp.stack(
        [
            lax.rem(y + (Y - s), Y) * CORE + (core if same else 1 - core)
            for s in range(Y)
            for same in (True, False)
        ]
    ).astype(jnp.int32)
    side = jnp.stack([x] + [lax.rem(x + (X - s), X) for s in shifts]).astype(jnp.int32)
    return project_output(order, side, mine, other, columns, expert_ids, router_logits)


def solution(mesh):
    fine = Mesh(mesh.devices.reshape(Z, X, Y, CORE), ("z", "x", "y", "core"))
    return jax.shard_map(
        local,
        mesh=fine,
        in_specs=(
            P(CTX, EXP),
            P(CTX, EXP),
            P(CTX, EXP),
            P(CTX, None),
            P(CTX, None),
            P(EXP, None, None),
            P(EXP, None, CTX),
        ),
        out_specs=P(CTX, EXP),
        check_vma=False,
    )
```

```python
import jax
import jax.numpy as jnp
from jax import lax
from jax.experimental import pallas as pl
from jax.experimental.pallas import tpu as pltpu
from jax.sharding import Mesh, PartitionSpec as P

QH = 4
HD = 128
Z, X, Y, CORE = 8, 4, 4, 2
EXPERTS = 8
TOK = 768
CAP = 216
STAT = 224
WIDE = 768
COLS = 192
SHIFTS = (2, 1, 3)
NEG = -1e30
SCALE2 = HD ** (-0.5) * 1.4426950408889634
F32 = jnp.float32
BF16 = jnp.bfloat16
CTX = ("z", "x")
EXP = ("y", "core")


def params(mebibytes=16):
    return pltpu.CompilerParams(vmem_limit_bytes=mebibytes * 1024 * 1024)


def whole(shape):
    return pl.BlockSpec(shape, lambda *_: (0,) * len(shape))


def nt(a, b):
    return lax.dot_general(a, b, (((1,), (1,)), ((), ())), preferred_element_type=F32)


def join_kernel(key_ref, value_ref, out_ref):
    out_ref[:, :HD] = key_ref[...]
    out_ref[:, HD:] = value_ref[...]


def join(keys, values):
    return pl.pallas_call(
        join_kernel,
        out_shape=jax.ShapeDtypeStruct((TOK, 2 * HD), BF16),
        compiler_params=params(60),
        name="join",
    )(keys, values)


def dispatch_kernel(
    ids_ref, tok_hbm, out_hbm, tok_ref, row_ref, load_sem, out_sems
):
    load = pltpu.make_async_copy(tok_hbm, tok_ref, load_sem)
    load.start()
    row = lax.broadcasted_iota(jnp.int32, (EXPERTS, TOK), 0)
    member = (ids_ref[0:1, :] == row) | (ids_ref[1:2, :] == row)
    before = lax.broadcasted_iota(jnp.int32, (TOK, TOK), 0) < lax.broadcasted_iota(
        jnp.int32, (TOK, TOK), 1
    )
    slots = jnp.dot(
        jnp.where(member, 1.0, 0.0).astype(BF16),
        jnp.where(before, 1.0, 0.0).astype(BF16),
        preferred_element_type=F32,
    )
    slots = jnp.where(member, slots, -1.0).astype(jnp.int32)
    load.wait()
    sends = []
    for e in range(EXPERTS):
        hit = lax.broadcasted_iota(jnp.int32, (CAP, TOK), 0) == slots[e : e + 1, :]
        row_ref[e] = jnp.dot(
            jnp.where(hit, 1.0, 0.0).astype(BF16), tok_ref[...], preferred_element_type=F32
        ).astype(BF16)
        send = pltpu.make_async_copy(row_ref.at[e], out_hbm.at[e], out_sems.at[e])
        send.start()
        sends.append(send)
    for send in sends:
        send.wait()


def dispatch(ids_t, tokens):
    return pl.pallas_call(
        dispatch_kernel,
        in_specs=[
            pl.BlockSpec(memory_space=pltpu.VMEM),
            pl.BlockSpec(memory_space=pltpu.HBM),
        ],
        out_specs=pl.BlockSpec(memory_space=pltpu.HBM),
        out_shape=jax.ShapeDtypeStruct((EXPERTS, CAP, WIDE), BF16),
        scratch_shapes=[
            pltpu.VMEM((TOK, WIDE), BF16),
            pltpu.VMEM((EXPERTS, CAP, WIDE), BF16),
            pltpu.SemaphoreType.DMA,
            pltpu.SemaphoreType.DMA((EXPERTS,)),
        ],
        cost_estimate=pl.CostEstimate(
            flops=2 * EXPERTS * CAP * TOK * WIDE,
            bytes_accessed=(EXPERTS * CAP + TOK) * WIDE * 2,
            transcendentals=0,
        ),
        compiler_params=params(60),
        name="dispatch",
    )(ids_t, tokens)


def prepare_kernel(me_ref, ids_ref, logit_ref, pos_ref, slot_ref, gate_ref):
    lane = lax.broadcasted_iota(jnp.int32, (TOK, HD), 1)
    first = ids_ref[:, 0:1] == lane
    second = ids_ref[:, 1:2] == lane
    member = first | second
    before = lax.broadcasted_iota(jnp.int32, (TOK, TOK), 1) < lax.broadcasted_iota(
        jnp.int32, (TOK, TOK), 0
    )
    slots = jnp.dot(
        jnp.where(before, 1.0, 0.0).astype(BF16),
        jnp.where(member, 1.0, 0.0).astype(BF16),
        preferred_element_type=F32,
    )
    slots = jnp.where(member, slots, -1.0)
    slot_ref[...] = slots
    l0, l1 = logit_ref[:, 0:1], logit_ref[:, 1:2]
    top = jnp.maximum(l0, l1)
    w0, w1 = jnp.exp(l0 - top), jnp.exp(l1 - top)
    total = w0 + w1
    gate_ref[...] = jnp.where(first, w0 / total, jnp.where(second, w1 / total, 0.0))
    mine = jnp.sum(jnp.where(lane == me_ref[0], slots, 0.0), axis=1, keepdims=True)
    hit = lax.broadcasted_iota(jnp.int32, (TOK, 256), 1) == mine.astype(jnp.int32)
    place = lax.broadcasted_iota(jnp.int32, (TOK, 256), 0).astype(F32)
    pos = jnp.max(jnp.where(hit, place, -1.0), axis=0, keepdims=True)
    pos = jnp.where(pos < 0.0, float(TOK - 1), pos)
    pos_ref[...] = jnp.broadcast_to(pos, (HD, 256)).T[:CAP, :]


def prepare(me, ids, logits):
    vmem = pl.BlockSpec(memory_space=pltpu.VMEM)
    return pl.pallas_call(
        prepare_kernel,
        in_specs=[pl.BlockSpec(memory_space=pltpu.SMEM), vmem, vmem],
        out_specs=[vmem] * 3,
        out_shape=[
            jax.ShapeDtypeStruct((CAP, HD), F32),
            jax.ShapeDtypeStruct((TOK, HD), F32),
            jax.ShapeDtypeStruct((TOK, HD), F32),
        ],
        compiler_params=params(),
        name="prepare",
    )(me, ids, logits)


def query_kernel(x_hbm, w_hbm, q_ref, x_ref, w_ref, sems):
    loads = []
    for j in range(EXPERTS):
        rows = pltpu.make_async_copy(x_hbm.at[j], x_ref.at[j], sems.at[0, j])
        weight = pltpu.make_async_copy(
            w_hbm.at[0, pl.ds(j * WIDE, WIDE), :], w_ref.at[j], sems.at[1, j]
        )
        rows.start()
        weight.start()
        loads.append((rows, weight))
    total = None
    for j, (rows, weight) in enumerate(loads):
        rows.wait()
        weight.wait()
        part = jnp.dot(x_ref[j], w_ref[j], preferred_element_type=F32)
        total = part if total is None else total + part
    for h in range(QH):
        q_ref[h] = total[:, h * HD : (h + 1) * HD].astype(BF16)


def project_queries(rows, weight):
    return pl.pallas_call(
        query_kernel,
        in_specs=[
            pl.BlockSpec(memory_space=pl.ANY),
            pl.BlockSpec(memory_space=pltpu.HBM),
        ],
        out_specs=pl.BlockSpec(memory_space=pltpu.VMEM),
        out_shape=jax.ShapeDtypeStruct((QH, CAP, HD), BF16),
        scratch_shapes=[
            pltpu.VMEM((EXPERTS, CAP, WIDE), BF16),
            pltpu.VMEM((EXPERTS, WIDE, QH * HD), BF16),
            pltpu.SemaphoreType.DMA((2, EXPERTS)),
        ],
        cost_estimate=pl.CostEstimate(
            flops=2 * EXPERTS * CAP * WIDE * QH * HD,
            bytes_accessed=EXPERTS * WIDE * (CAP + QH * HD) * 2,
            transcendentals=0,
        ),
        compiler_params=params(50),
        name="queries",
    )(rows, weight)


def attend_kernel(masked, place_ref, own_ref, q_ref, pos_ref, kv_hbm, out_ref, kv_ref, top_ref, acc_ref, sems):
    z = place_ref[0]

    def wanted(i):
        return pl.when(i < z) if i < Z - 1 else pl.when(own_ref[0] > 0)

    loads = [
        pltpu.make_async_copy(kv_hbm.at[i if i < Z - 1 else z], kv_ref.at[i], sems.at[i])
        for i in range(Z)
    ]
    for i in range(Z):
        wanted(i)(lambda i=i: loads[i].start())
    top_ref[...] = jnp.full(top_ref.shape, NEG, F32)
    acc_ref[...] = jnp.zeros(acc_ref.shape, F32)

    def block(i):
        mask = masked and i == Z - 1
        loads[i].wait()
        k = kv_ref[i, :, :HD]
        v = jnp.concatenate([kv_ref[i, :, HD:], jnp.ones((TOK, HD), BF16)], axis=1)
        scores = [nt(q_ref[h], k) for h in range(QH)]
        for h in range(QH):
            s = scores[h]
            if mask:
                place = lax.broadcasted_iota(jnp.int32, (CAP, TOK), 1).astype(F32)
                s = jnp.where(place <= pos_ref[:, 0:1], s, NEG)
            old = top_ref[h]
            new = jnp.maximum(old, jnp.max(s, axis=1, keepdims=True))
            p = jnp.exp2((s - jnp.concatenate([new] * (TOK // 128), axis=1)) * SCALE2)
            shrink = jnp.exp2((old - new) * SCALE2)
            acc_ref[h] = acc_ref[h] * jnp.concatenate([shrink, shrink], axis=1) + jnp.dot(
                p.astype(BF16), v, preferred_element_type=F32
            )
            top_ref[h] = new

    for i in range(Z):
        wanted(i)(lambda i=i: block(i))

    for h in range(QH):
        total = acc_ref[h, :, HD:]
        some = total > 0.0
        safe = jnp.where(some, total, 1.0)
        out_ref[h, :CAP, :] = (acc_ref[h, :, :HD] / safe).astype(BF16)
        out_ref[h, CAP:STAT, :] = jnp.zeros((STAT - CAP, HD), BF16)
        stat = jnp.where(some, top_ref[h] * SCALE2 + jnp.log2(safe), NEG)
        stat = jnp.concatenate([stat, jnp.zeros((256 - CAP, HD), F32)], axis=0).T[0:16, :]
        line = lax.broadcasted_iota(jnp.int32, (16, HD), 0)
        spread = jnp.where(lax.rem(line, 2) == 0, stat[:, :HD], stat[:, HD:])
        high = spread.astype(BF16).astype(F32)
        middle = (spread - high).astype(BF16).astype(F32)
        low = spread - high - middle
        parts = jnp.where(line < 2, high, jnp.where(line < 4, middle, low))
        out_ref[h, STAT:, :] = parts.astype(BF16)


def attend(masked, place, own, q, pos, blocks):
    name = "attend_own" if masked else "attend_near"
    return pl.pallas_call(
        lambda *refs: attend_kernel(masked, *refs),
        in_specs=[pl.BlockSpec(memory_space=pltpu.SMEM)] * 2
        + [pl.BlockSpec(memory_space=pltpu.VMEM)] * 2
        + [pl.BlockSpec(memory_space=pl.ANY)],
        out_specs=pl.BlockSpec(memory_space=pltpu.VMEM),
        out_shape=jax.ShapeDtypeStruct((QH, STAT + 16, HD), BF16),
        scratch_shapes=[
            pltpu.VMEM((Z, TOK, 2 * HD), BF16),
            pltpu.VMEM((QH, CAP, HD), F32),
            pltpu.VMEM((QH, CAP, 2 * HD), F32),
            pltpu.SemaphoreType.DMA((Z,)),
        ],
        cost_estimate=pl.CostEstimate(
            flops=4 * QH * CAP * HD * 4 * TOK,
            bytes_accessed=8 * TOK * 2 * HD * 2,
            transcendentals=QH * CAP * 4 * TOK,
        ),
        compiler_params=params(),
        name=name,
    )(place, own, q, pos, blocks)


def combine_kernel(*refs):
    outs, out_ref = refs[:4], refs[4]
    for h in range(QH):
        logs = []
        for o in outs:
            parts = o[h, STAT:, :].astype(F32)
            even = parts[0:1] + parts[2:3] + parts[4:5]
            odd = parts[1:2] + parts[3:4] + parts[5:6]
            stat = jnp.concatenate([even, odd], axis=1)
            logs.append(jnp.broadcast_to(stat, (HD, 256)).T[:CAP, :])
        top = jnp.maximum(jnp.maximum(logs[0], logs[1]), jnp.maximum(logs[2], logs[3]))
        weights = [jnp.exp2(v - top) for v in logs]
        total = weights[0] + weights[1] + weights[2] + weights[3]
        summed = sum(w * o[h, :CAP, :].astype(F32) for w, o in zip(weights, outs))
        out_ref[:, h * HD : (h + 1) * HD] = (summed / total).astype(BF16)


def combine(outs):
    return pl.pallas_call(
        combine_kernel,
        out_shape=jax.ShapeDtypeStruct((CAP, QH * HD), BF16),
        compiler_params=params(),
        name="combine",
    )(*outs)


def output_kernel(
    place_ref, mine_ref, other_ref, w_hbm, slot_ref, gate_ref, out_ref, w_ref, acc_ref, sems
):
    x, y, core = place_ref[1], place_ref[2], place_ref[3]
    order = [
        lax.rem(y + (Y - j // 2), Y) * CORE + (core if j % 2 == 0 else 1 - core)
        for j in range(EXPERTS)
    ]
    held = [lax.rem(e + y * CORE + core, Z) for e in order]
    sides = [x] + [lax.rem(x + (X - s), X) for s in SHIFTS]
    loads = [
        [
            pltpu.make_async_copy(
                w_hbm.at[held[j], i],
                w_ref.at[j, pl.ds(pl.multiple_of(sides[i] * COLS, COLS), COLS), :],
                sems.at[j, i],
            )
            for i in range(X)
        ]
        for j in range(EXPERTS)
    ]
    for group in loads:
        for load in group:
            load.start()
    lane = lax.broadcasted_iota(jnp.int32, (TOK, HD), 1)
    for j in range(EXPERTS):
        rows = (mine_ref if j % 2 == 0 else other_ref)[j // 2]
        here = lane == order[j]
        slot = jnp.sum(jnp.where(here, slot_ref[...], 0.0), axis=1, keepdims=True).astype(jnp.int32)
        gate = jnp.sum(jnp.where(here, gate_ref[...], 0.0), axis=1, keepdims=True)
        hit = lax.broadcasted_iota(jnp.int32, (TOK, CAP), 1) == slot
        spread = jnp.where(hit, gate, 0.0).astype(BF16)
        for load in loads[j]:
            load.wait()
        projected = nt(rows, w_ref[j]).astype(BF16)
        part = jnp.dot(spread, projected, preferred_element_type=F32)
        if j == 0:
            acc_ref[...] = part
        elif j < EXPERTS - 1:
            acc_ref[...] += part
        else:
            out_ref[...] = (acc_ref[...] + part).astype(BF16)


def project_output(place, mine, other, weight, slots, gates):
    vmem = pl.BlockSpec(memory_space=pltpu.VMEM)
    return pl.pallas_call(
        output_kernel,
        in_specs=[
            pl.BlockSpec(memory_space=pltpu.SMEM),
            vmem,
            vmem,
            pl.BlockSpec(memory_space=pltpu.HBM),
            vmem,
            vmem,
        ],
        out_specs=vmem,
        out_shape=jax.ShapeDtypeStruct((TOK, WIDE), BF16),
        scratch_shapes=[
            pltpu.VMEM((EXPERTS, WIDE, QH * HD), BF16),
            pltpu.VMEM((TOK, WIDE), F32),
            pltpu.SemaphoreType.DMA((EXPERTS, X)),
        ],
        cost_estimate=pl.CostEstimate(
            flops=2 * EXPERTS * CAP * WIDE * (QH * HD + TOK),
            bytes_accessed=EXPERTS * WIDE * QH * HD * 2,
            transcendentals=0,
        ),
        compiler_params=params(48),
        name="output",
    )(place, mine, other, weight, slots, gates)


def turn(n, by):
    return [(i, (i + by) % n) for i in range(n)]


def local(tokens, keys, values, expert_ids, router_logits, query_weight, output_weight):
    z = lax.axis_index("z")
    x = lax.axis_index("x")
    y = lax.axis_index("y")
    core = lax.axis_index("core")
    me = y * CORE + core
    place = jnp.stack([z, x, y, core]).astype(jnp.int32)

    blocks = lax.all_gather(join(keys, values), "z", axis=0)

    piece = output_weight[0].T
    piece = lax.ppermute(
        piece,
        CTX + EXP,
        [
            ((i * X + j) * EXPERTS + e, ((i + e) % Z * X + j) * EXPERTS + e)
            for i in range(Z)
            for j in range(X)
            for e in range(EXPERTS)
        ],
    )
    piece = lax.ppermute(
        piece,
        CTX + EXP,
        [
            ((i * X + j) * EXPERTS + e, (i * X + j) * EXPERTS + (i - e) % EXPERTS)
            for i in range(Z)
            for j in range(X)
            for e in range(EXPERTS)
        ],
    )
    pieces = [piece] + [lax.ppermute(piece, "x", turn(X, s)) for s in SHIFTS]

    outgoing = dispatch(expert_ids.T, tokens)
    prepared = prepare(me[None].astype(jnp.int32), expert_ids, router_logits)
    incoming = lax.all_to_all(outgoing, EXP, split_axis=0, concat_axis=0, tiled=True)
    pieces, incoming, (pos, slots, gates), place = lax.optimization_barrier(
        (jnp.stack(pieces), incoming, prepared, place)
    )
    columns = lax.all_gather(pieces, "z", axis=0)
    q = project_queries(incoming, query_weight)

    theirs = [lax.ppermute(q, "x", turn(X, s)) for s in SHIFTS]
    outs = [attend(True, place, jnp.ones((1,), jnp.int32), q, pos, blocks)]
    theirs, _ = lax.optimization_barrier((theirs, outs[0]))
    for s, other in zip(SHIFTS, theirs):
        source = lax.rem(x + (X - s), X)
        o = attend(False, place, (x < source)[None].astype(jnp.int32), other, pos, blocks)
        outs.append(lax.ppermute(o, "x", turn(X, X - s)))
    attended = combine(outs)

    near = [lax.ppermute(attended, "y", turn(Y, s)) for s in range(1, Y)]
    mine = jnp.stack([attended] + near)
    other = lax.ppermute(mine, "core", [(0, 1), (1, 0)])
    return project_output(place, mine, other, columns, slots, gates)


def solution(mesh):
    fine = Mesh(mesh.devices.reshape(Z, X, Y, CORE), ("z", "x", "y", "core"))
    return jax.shard_map(
        local,
        mesh=fine,
        in_specs=(
            P(CTX, EXP),
            P(CTX, EXP),
            P(CTX, EXP),
            P(CTX, None),
            P(CTX, None),
            P(EXP, None, None),
            P(EXP, None, CTX),
        ),
        out_specs=P(CTX, EXP),
        check_vma=False,
    )
```

```python
import jax
import jax.numpy as jnp
from jax import lax
from jax.experimental import pallas as pl
from jax.experimental.pallas import tpu as pltpu
from jax.sharding import Mesh, PartitionSpec as P

QH = 4
HD = 128
Z, X, Y, CORE = 8, 4, 4, 2
EXPERTS = 8
TOK = 768
CAP = 216
STAT = 224
WIDE = 768
COLS = 192
SHIFTS = (2, 1, 3)
NEG = -1e30
SCALE2 = HD ** (-0.5) * 1.4426950408889634
F32 = jnp.float32
BF16 = jnp.bfloat16
CTX = ("z", "x")
EXP = ("y", "core")


def params(mebibytes=16):
    return pltpu.CompilerParams(vmem_limit_bytes=mebibytes * 1024 * 1024)


def whole(shape):
    return pl.BlockSpec(shape, lambda *_: (0,) * len(shape))


def nt(a, b):
    return lax.dot_general(a, b, (((1,), (1,)), ((), ())), preferred_element_type=F32)


def join_kernel(key_ref, value_ref, out_ref):
    out_ref[:, :HD] = key_ref[...]
    out_ref[:, HD:] = value_ref[...]


def join(keys, values):
    return pl.pallas_call(
        join_kernel,
        out_shape=jax.ShapeDtypeStruct((TOK, 2 * HD), BF16),
        compiler_params=params(60),
        name="join",
    )(keys, values)


def dispatch_kernel(
    ids_ref, tok_hbm, out_hbm, tok_ref, row_ref, load_sem, out_sems
):
    load = pltpu.make_async_copy(tok_hbm, tok_ref, load_sem)
    load.start()
    row = lax.broadcasted_iota(jnp.int32, (EXPERTS, TOK), 0)
    member = (ids_ref[0:1, :] == row) | (ids_ref[1:2, :] == row)
    before = lax.broadcasted_iota(jnp.int32, (TOK, TOK), 0) < lax.broadcasted_iota(
        jnp.int32, (TOK, TOK), 1
    )
    slots = jnp.dot(
        jnp.where(member, 1.0, 0.0).astype(BF16),
        jnp.where(before, 1.0, 0.0).astype(BF16),
        preferred_element_type=F32,
    )
    slots = jnp.where(member, slots, -1.0).astype(jnp.int32)
    load.wait()
    sends = []
    for e in range(EXPERTS):
        hit = lax.broadcasted_iota(jnp.int32, (CAP, TOK), 0) == slots[e : e + 1, :]
        row_ref[e] = jnp.dot(
            jnp.where(hit, 1.0, 0.0).astype(BF16), tok_ref[...], preferred_element_type=F32
        ).astype(BF16)
        send = pltpu.make_async_copy(row_ref.at[e], out_hbm.at[e], out_sems.at[e])
        send.start()
        sends.append(send)
    for send in sends:
        send.wait()


def dispatch(ids_t, tokens):
    return pl.pallas_call(
        dispatch_kernel,
        in_specs=[
            pl.BlockSpec(memory_space=pltpu.VMEM),
            pl.BlockSpec(memory_space=pltpu.HBM),
        ],
        out_specs=pl.BlockSpec(memory_space=pltpu.HBM),
        out_shape=jax.ShapeDtypeStruct((EXPERTS, CAP, WIDE), BF16),
        scratch_shapes=[
            pltpu.VMEM((TOK, WIDE), BF16),
            pltpu.VMEM((EXPERTS, CAP, WIDE), BF16),
            pltpu.SemaphoreType.DMA,
            pltpu.SemaphoreType.DMA((EXPERTS,)),
        ],
        cost_estimate=pl.CostEstimate(
            flops=2 * EXPERTS * CAP * TOK * WIDE,
            bytes_accessed=(EXPERTS * CAP + TOK) * WIDE * 2,
            transcendentals=0,
        ),
        compiler_params=params(60),
        name="dispatch",
    )(ids_t, tokens)


def prepare_kernel(me_ref, ids_ref, logit_ref, pos_ref, slot_ref, gate_ref):
    lane = lax.broadcasted_iota(jnp.int32, (TOK, HD), 1)
    first = ids_ref[:, 0:1] == lane
    second = ids_ref[:, 1:2] == lane
    member = first | second
    before = lax.broadcasted_iota(jnp.int32, (TOK, TOK), 1) < lax.broadcasted_iota(
        jnp.int32, (TOK, TOK), 0
    )
    slots = jnp.dot(
        jnp.where(before, 1.0, 0.0).astype(BF16),
        jnp.where(member, 1.0, 0.0).astype(BF16),
        preferred_element_type=F32,
    )
    slots = jnp.where(member, slots, -1.0)
    slot_ref[...] = slots
    l0, l1 = logit_ref[:, 0:1], logit_ref[:, 1:2]
    top = jnp.maximum(l0, l1)
    w0, w1 = jnp.exp(l0 - top), jnp.exp(l1 - top)
    total = w0 + w1
    gate_ref[...] = jnp.where(first, w0 / total, jnp.where(second, w1 / total, 0.0))
    mine = jnp.sum(jnp.where(lane == me_ref[0], slots, 0.0), axis=1, keepdims=True)
    hit = lax.broadcasted_iota(jnp.int32, (TOK, 256), 1) == mine.astype(jnp.int32)
    place = lax.broadcasted_iota(jnp.int32, (TOK, 256), 0).astype(F32)
    pos = jnp.max(jnp.where(hit, place, -1.0), axis=0, keepdims=True)
    pos = jnp.where(pos < 0.0, float(TOK - 1), pos)
    pos_ref[...] = jnp.broadcast_to(pos, (HD, 256)).T[:CAP, :]


def prepare(me, ids, logits):
    vmem = pl.BlockSpec(memory_space=pltpu.VMEM)
    return pl.pallas_call(
        prepare_kernel,
        in_specs=[pl.BlockSpec(memory_space=pltpu.SMEM), vmem, vmem],
        out_specs=[vmem] * 3,
        out_shape=[
            jax.ShapeDtypeStruct((CAP, HD), F32),
            jax.ShapeDtypeStruct((TOK, HD), F32),
            jax.ShapeDtypeStruct((TOK, HD), F32),
        ],
        compiler_params=params(),
        name="prepare",
    )(me, ids, logits)


def query_kernel(x_hbm, w_hbm, q_ref, x_ref, w_ref, sems):
    loads = []
    for j in range(EXPERTS):
        rows = pltpu.make_async_copy(x_hbm.at[j], x_ref.at[j], sems.at[0, j])
        weight = pltpu.make_async_copy(
            w_hbm.at[0, pl.ds(j * WIDE, WIDE), :], w_ref.at[j], sems.at[1, j]
        )
        rows.start()
        weight.start()
        loads.append((rows, weight))
    total = None
    for j, (rows, weight) in enumerate(loads):
        rows.wait()
        weight.wait()
        part = jnp.dot(x_ref[j], w_ref[j], preferred_element_type=F32)
        total = part if total is None else total + part
    for h in range(QH):
        q_ref[h] = total[:, h * HD : (h + 1) * HD].astype(BF16)


def project_queries(rows, weight):
    return pl.pallas_call(
        query_kernel,
        in_specs=[
            pl.BlockSpec(memory_space=pl.ANY),
            pl.BlockSpec(memory_space=pltpu.HBM),
        ],
        out_specs=pl.BlockSpec(memory_space=pltpu.VMEM),
        out_shape=jax.ShapeDtypeStruct((QH, CAP, HD), BF16),
        scratch_shapes=[
            pltpu.VMEM((EXPERTS, CAP, WIDE), BF16),
            pltpu.VMEM((EXPERTS, WIDE, QH * HD), BF16),
            pltpu.SemaphoreType.DMA((2, EXPERTS)),
        ],
        cost_estimate=pl.CostEstimate(
            flops=2 * EXPERTS * CAP * WIDE * QH * HD,
            bytes_accessed=EXPERTS * WIDE * (CAP + QH * HD) * 2,
            transcendentals=0,
        ),
        compiler_params=params(50),
        name="queries",
    )(rows, weight)


def attend_kernel(masked, place_ref, own_ref, q_ref, pos_ref, kv_hbm, out_ref, kv_ref, top_ref, acc_ref, sems):
    z = place_ref[0]

    def wanted(i):
        return pl.when(i < z) if i < Z - 1 else pl.when(own_ref[0] > 0)

    loads = [
        pltpu.make_async_copy(kv_hbm.at[i if i < Z - 1 else z], kv_ref.at[i], sems.at[i])
        for i in range(Z)
    ]
    for i in range(Z):
        wanted(i)(lambda i=i: loads[i].start())
    top_ref[...] = jnp.full(top_ref.shape, NEG, F32)
    acc_ref[...] = jnp.zeros(acc_ref.shape, F32)

    def block(i):
        mask = masked and i == Z - 1
        loads[i].wait()
        k = kv_ref[i, :, :HD]
        v = jnp.concatenate([kv_ref[i, :, HD:], jnp.ones((TOK, HD), BF16)], axis=1)
        scores = [nt(q_ref[h], k) for h in range(QH)]
        for h in range(QH):
            s = scores[h]
            if mask:
                place = lax.broadcasted_iota(jnp.int32, (CAP, TOK), 1).astype(F32)
                s = jnp.where(place <= pos_ref[:, 0:1], s, NEG)
            old = top_ref[h]
            new = jnp.maximum(old, jnp.max(s, axis=1, keepdims=True))
            p = jnp.exp2((s - jnp.concatenate([new] * (TOK // 128), axis=1)) * SCALE2)
            shrink = jnp.exp2((old - new) * SCALE2)
            acc_ref[h] = acc_ref[h] * jnp.concatenate([shrink, shrink], axis=1) + jnp.dot(
                p.astype(BF16), v, preferred_element_type=F32
            )
            top_ref[h] = new

    for i in range(Z):
        wanted(i)(lambda i=i: block(i))

    for h in range(QH):
        total = acc_ref[h, :, HD:]
        some = total > 0.0
        safe = jnp.where(some, total, 1.0)
        out_ref[h, :CAP, :] = (acc_ref[h, :, :HD] / safe).astype(BF16)
        out_ref[h, CAP:STAT, :] = jnp.zeros((STAT - CAP, HD), BF16)
        stat = jnp.where(some, top_ref[h] * SCALE2 + jnp.log2(safe), NEG)
        stat = jnp.concatenate([stat, jnp.zeros((256 - CAP, HD), F32)], axis=0).T[0:16, :]
        line = lax.broadcasted_iota(jnp.int32, (16, HD), 0)
        spread = jnp.where(lax.rem(line, 2) == 0, stat[:, :HD], stat[:, HD:])
        high = spread.astype(BF16).astype(F32)
        middle = (spread - high).astype(BF16).astype(F32)
        low = spread - high - middle
        parts = jnp.where(line < 2, high, jnp.where(line < 4, middle, low))
        out_ref[h, STAT:, :] = parts.astype(BF16)


def attend(masked, place, own, q, pos, blocks):
    name = "attend_own" if masked else "attend_near"
    return pl.pallas_call(
        lambda *refs: attend_kernel(masked, *refs),
        in_specs=[pl.BlockSpec(memory_space=pltpu.SMEM)] * 2
        + [pl.BlockSpec(memory_space=pltpu.VMEM)] * 2
        + [pl.BlockSpec(memory_space=pl.ANY)],
        out_specs=pl.BlockSpec(memory_space=pltpu.VMEM),
        out_shape=jax.ShapeDtypeStruct((QH, STAT + 16, HD), BF16),
        scratch_shapes=[
            pltpu.VMEM((Z, TOK, 2 * HD), BF16),
            pltpu.VMEM((QH, CAP, HD), F32),
            pltpu.VMEM((QH, CAP, 2 * HD), F32),
            pltpu.SemaphoreType.DMA((Z,)),
        ],
        cost_estimate=pl.CostEstimate(
            flops=4 * QH * CAP * HD * 4 * TOK,
            bytes_accessed=8 * TOK * 2 * HD * 2,
            transcendentals=QH * CAP * 4 * TOK,
        ),
        compiler_params=params(),
        name=name,
    )(place, own, q, pos, blocks)


def combine_kernel(*refs):
    outs, out_ref = refs[:4], refs[4]
    for h in range(QH):
        logs = []
        for o in outs:
            parts = o[h, STAT:, :].astype(F32)
            even = parts[0:1] + parts[2:3] + parts[4:5]
            odd = parts[1:2] + parts[3:4] + parts[5:6]
            stat = jnp.concatenate([even, odd], axis=1)
            logs.append(jnp.broadcast_to(stat, (HD, 256)).T[:CAP, :])
        top = jnp.maximum(jnp.maximum(logs[0], logs[1]), jnp.maximum(logs[2], logs[3]))
        weights = [jnp.exp2(v - top) for v in logs]
        total = weights[0] + weights[1] + weights[2] + weights[3]
        summed = sum(w * o[h, :CAP, :].astype(F32) for w, o in zip(weights, outs))
        out_ref[:, h * HD : (h + 1) * HD] = (summed / total).astype(BF16)


def combine(outs):
    return pl.pallas_call(
        combine_kernel,
        out_shape=jax.ShapeDtypeStruct((CAP, QH * HD), BF16),
        compiler_params=params(),
        name="combine",
    )(*outs)


def output_kernel(
    place_ref, mine_ref, other_ref, w_hbm, slot_ref, gate_ref, out_ref, w_ref, acc_ref, sems
):
    x, y, core = place_ref[1], place_ref[2], place_ref[3]
    order = [
        lax.rem(y + (Y - j // 2), Y) * CORE + (core if j % 2 == 0 else 1 - core)
        for j in range(EXPERTS)
    ]
    held = [lax.rem(e + y * CORE + core, Z) for e in order]
    sides = [x] + [lax.rem(x + (X - s), X) for s in SHIFTS]
    loads = [
        [
            pltpu.make_async_copy(
                w_hbm.at[held[j], i],
                w_ref.at[j, pl.ds(pl.multiple_of(sides[i] * COLS, COLS), COLS), :],
                sems.at[j, i],
            )
            for i in range(X)
        ]
        for j in range(EXPERTS)
    ]
    for group in loads:
        for load in group:
            load.start()
    lane = lax.broadcasted_iota(jnp.int32, (TOK, HD), 1)
    for j in range(EXPERTS):
        rows = (mine_ref if j % 2 == 0 else other_ref)[j // 2]
        here = lane == order[j]
        slot = jnp.sum(jnp.where(here, slot_ref[...], 0.0), axis=1, keepdims=True).astype(jnp.int32)
        gate = jnp.sum(jnp.where(here, gate_ref[...], 0.0), axis=1, keepdims=True)
        hit = lax.broadcasted_iota(jnp.int32, (TOK, CAP), 1) == slot
        spread = jnp.where(hit, gate, 0.0).astype(BF16)
        for load in loads[j]:
            load.wait()
        projected = nt(rows, w_ref[j]).astype(BF16)
        part = jnp.dot(spread, projected, preferred_element_type=F32)
        if j == 0:
            acc_ref[...] = part
        elif j < EXPERTS - 1:
            acc_ref[...] += part
        else:
            out_ref[...] = (acc_ref[...] + part).astype(BF16)


def project_output(place, mine, other, weight, slots, gates):
    vmem = pl.BlockSpec(memory_space=pltpu.VMEM)
    return pl.pallas_call(
        output_kernel,
        in_specs=[
            pl.BlockSpec(memory_space=pltpu.SMEM),
            vmem,
            vmem,
            pl.BlockSpec(memory_space=pltpu.HBM),
            vmem,
            vmem,
        ],
        out_specs=vmem,
        out_shape=jax.ShapeDtypeStruct((TOK, WIDE), BF16),
        scratch_shapes=[
            pltpu.VMEM((EXPERTS, WIDE, QH * HD), BF16),
            pltpu.VMEM((TOK, WIDE), F32),
            pltpu.SemaphoreType.DMA((EXPERTS, X)),
        ],
        cost_estimate=pl.CostEstimate(
            flops=2 * EXPERTS * CAP * WIDE * (QH * HD + TOK),
            bytes_accessed=EXPERTS * WIDE * QH * HD * 2,
            transcendentals=0,
        ),
        compiler_params=params(48),
        name="output",
    )(place, mine, other, weight, slots, gates)


def turn(n, by):
    return [(i, (i + by) % n) for i in range(n)]


def local(tokens, keys, values, expert_ids, router_logits, query_weight, output_weight):
    z = lax.axis_index("z")
    x = lax.axis_index("x")
    y = lax.axis_index("y")
    core = lax.axis_index("core")
    me = y * CORE + core
    place = jnp.stack([z, x, y, core]).astype(jnp.int32)

    blocks = lax.all_gather(join(keys, values), "z", axis=0)

    piece = lax.ppermute(
        output_weight[0].T,
        CTX + EXP,
        [
            ((i * X + j) * EXPERTS + e, ((i + e) % Z * X + j) * EXPERTS + i)
            for i in range(Z)
            for j in range(X)
            for e in range(EXPERTS)
        ],
    )
    pieces = [piece] + [lax.ppermute(piece, "x", turn(X, s)) for s in SHIFTS]

    outgoing = dispatch(expert_ids.T, tokens)
    prepared = prepare(me[None].astype(jnp.int32), expert_ids, router_logits)
    incoming = lax.all_to_all(outgoing, EXP, split_axis=0, concat_axis=0, tiled=True)
    incoming, (pos, slots, gates), place = lax.optimization_barrier((incoming, prepared, place))
    q = project_queries(incoming, query_weight)
    pieces, _ = lax.optimization_barrier((pieces, q))
    columns = lax.all_gather(jnp.stack(pieces), "z", axis=0)

    theirs = [lax.ppermute(q, "x", turn(X, s)) for s in SHIFTS]
    outs = [attend(True, place, jnp.ones((1,), jnp.int32), q, pos, blocks)]
    theirs, _ = lax.optimization_barrier((theirs, outs[0]))
    for s, other in zip(SHIFTS, theirs):
        source = lax.rem(x + (X - s), X)
        o = attend(False, place, (x < source)[None].astype(jnp.int32), other, pos, blocks)
        outs.append(lax.ppermute(o, "x", turn(X, X - s)))
    attended = combine(outs)

    near = [lax.ppermute(attended, "y", turn(Y, s)) for s in range(1, Y)]
    mine = jnp.stack([attended] + near)
    other = lax.ppermute(mine, "core", [(0, 1), (1, 0)])
    return project_output(place, mine, other, columns, slots, gates)


def solution(mesh):
    fine = Mesh(mesh.devices.reshape(Z, X, Y, CORE), ("z", "x", "y", "core"))
    return jax.shard_map(
        local,
        mesh=fine,
        in_specs=(
            P(CTX, EXP),
            P(CTX, EXP),
            P(CTX, EXP),
            P(CTX, None),
            P(CTX, None),
            P(EXP, None, None),
            P(EXP, None, CTX),
        ),
        out_specs=P(CTX, EXP),
        check_vma=False,
    )
```

```python
import jax
import jax.numpy as jnp
from jax import lax
from jax.experimental import pallas as pl
from jax.experimental.pallas import tpu as pltpu
from jax.sharding import Mesh, PartitionSpec as P

QH = 4
HD = 128
Z, X, Y, CORE = 8, 4, 4, 2
EXPERTS = 8
TOK = 768
CAP = 216
STAT = 224
WIDE = 768
COLS = 192
SHIFTS = (1, 3, 2)
NEG = -1e30
SCALE2 = HD ** (-0.5) * 1.4426950408889634
F32 = jnp.float32
BF16 = jnp.bfloat16
CTX = ("z", "x")
EXP = ("y", "core")


def params(mebibytes=16):
    return pltpu.CompilerParams(vmem_limit_bytes=mebibytes * 1024 * 1024)


def whole(shape):
    return pl.BlockSpec(shape, lambda *_: (0,) * len(shape))


def nt(a, b):
    return lax.dot_general(a, b, (((1,), (1,)), ((), ())), preferred_element_type=F32)


def join_kernel(key_ref, value_ref, out_ref):
    out_ref[:, :HD] = key_ref[...]
    out_ref[:, HD:] = value_ref[...]


def join(keys, values):
    return pl.pallas_call(
        join_kernel,
        out_shape=jax.ShapeDtypeStruct((TOK, 2 * HD), BF16),
        compiler_params=params(60),
        name="join",
    )(keys, values)


def dispatch_kernel(
    ids_ref, tok_hbm, out_hbm, tok_ref, row_ref, load_sem, out_sems
):
    load = pltpu.make_async_copy(tok_hbm, tok_ref, load_sem)
    load.start()
    row = lax.broadcasted_iota(jnp.int32, (EXPERTS, TOK), 0)
    member = (ids_ref[0:1, :] == row) | (ids_ref[1:2, :] == row)
    before = lax.broadcasted_iota(jnp.int32, (TOK, TOK), 0) < lax.broadcasted_iota(
        jnp.int32, (TOK, TOK), 1
    )
    slots = jnp.dot(
        jnp.where(member, 1.0, 0.0).astype(BF16),
        jnp.where(before, 1.0, 0.0).astype(BF16),
        preferred_element_type=F32,
    )
    slots = jnp.where(member, slots, -1.0).astype(jnp.int32)
    load.wait()
    sends = []
    for e in range(EXPERTS):
        hit = lax.broadcasted_iota(jnp.int32, (CAP, TOK), 0) == slots[e : e + 1, :]
        row_ref[e] = jnp.dot(
            jnp.where(hit, 1.0, 0.0).astype(BF16), tok_ref[...], preferred_element_type=F32
        ).astype(BF16)
        send = pltpu.make_async_copy(row_ref.at[e], out_hbm.at[e], out_sems.at[e])
        send.start()
        sends.append(send)
    for send in sends:
        send.wait()


def dispatch(ids_t, tokens):
    return pl.pallas_call(
        dispatch_kernel,
        in_specs=[
            pl.BlockSpec(memory_space=pltpu.VMEM),
            pl.BlockSpec(memory_space=pltpu.HBM),
        ],
        out_specs=pl.BlockSpec(memory_space=pltpu.HBM),
        out_shape=jax.ShapeDtypeStruct((EXPERTS, CAP, WIDE), BF16),
        scratch_shapes=[
            pltpu.VMEM((TOK, WIDE), BF16),
            pltpu.VMEM((EXPERTS, CAP, WIDE), BF16),
            pltpu.SemaphoreType.DMA,
            pltpu.SemaphoreType.DMA((EXPERTS,)),
        ],
        cost_estimate=pl.CostEstimate(
            flops=2 * EXPERTS * CAP * TOK * WIDE,
            bytes_accessed=(EXPERTS * CAP + TOK) * WIDE * 2,
            transcendentals=0,
        ),
        compiler_params=params(60),
        name="dispatch",
    )(ids_t, tokens)


def prepare_kernel(me_ref, ids_ref, logit_ref, pos_ref, slot_ref, gate_ref):
    lane = lax.broadcasted_iota(jnp.int32, (TOK, HD), 1)
    first = ids_ref[:, 0:1] == lane
    second = ids_ref[:, 1:2] == lane
    member = first | second
    before = lax.broadcasted_iota(jnp.int32, (TOK, TOK), 1) < lax.broadcasted_iota(
        jnp.int32, (TOK, TOK), 0
    )
    slots = jnp.dot(
        jnp.where(before, 1.0, 0.0).astype(BF16),
        jnp.where(member, 1.0, 0.0).astype(BF16),
        preferred_element_type=F32,
    )
    slots = jnp.where(member, slots, -1.0)
    slot_ref[...] = slots
    l0, l1 = logit_ref[:, 0:1], logit_ref[:, 1:2]
    top = jnp.maximum(l0, l1)
    w0, w1 = jnp.exp(l0 - top), jnp.exp(l1 - top)
    total = w0 + w1
    gate_ref[...] = jnp.where(first, w0 / total, jnp.where(second, w1 / total, 0.0))
    mine = jnp.sum(jnp.where(lane == me_ref[0], slots, 0.0), axis=1, keepdims=True)
    hit = lax.broadcasted_iota(jnp.int32, (TOK, 256), 1) == mine.astype(jnp.int32)
    place = lax.broadcasted_iota(jnp.int32, (TOK, 256), 0).astype(F32)
    pos = jnp.max(jnp.where(hit, place, -1.0), axis=0, keepdims=True)
    pos = jnp.where(pos < 0.0, float(TOK - 1), pos)
    pos_ref[...] = jnp.broadcast_to(pos, (HD, 256)).T[:CAP, :]


def prepare(me, ids, logits):
    vmem = pl.BlockSpec(memory_space=pltpu.VMEM)
    return pl.pallas_call(
        prepare_kernel,
        in_specs=[pl.BlockSpec(memory_space=pltpu.SMEM), vmem, vmem],
        out_specs=[vmem] * 3,
        out_shape=[
            jax.ShapeDtypeStruct((CAP, HD), F32),
            jax.ShapeDtypeStruct((TOK, HD), F32),
            jax.ShapeDtypeStruct((TOK, HD), F32),
        ],
        compiler_params=params(),
        name="prepare",
    )(me, ids, logits)


def query_kernel(x_hbm, w_hbm, q_ref, x_ref, w_ref, sems):
    loads = []
    for j in range(EXPERTS):
        rows = pltpu.make_async_copy(x_hbm.at[j], x_ref.at[j], sems.at[0, j])
        weight = pltpu.make_async_copy(
            w_hbm.at[0, pl.ds(j * WIDE, WIDE), :], w_ref.at[j], sems.at[1, j]
        )
        rows.start()
        weight.start()
        loads.append((rows, weight))
    total = None
    for j, (rows, weight) in enumerate(loads):
        rows.wait()
        weight.wait()
        part = jnp.dot(x_ref[j], w_ref[j], preferred_element_type=F32)
        total = part if total is None else total + part
    for h in range(QH):
        q_ref[h] = total[:, h * HD : (h + 1) * HD].astype(BF16)


def project_queries(rows, weight):
    return pl.pallas_call(
        query_kernel,
        in_specs=[
            pl.BlockSpec(memory_space=pl.ANY),
            pl.BlockSpec(memory_space=pltpu.HBM),
        ],
        out_specs=pl.BlockSpec(memory_space=pltpu.VMEM),
        out_shape=jax.ShapeDtypeStruct((QH, CAP, HD), BF16),
        scratch_shapes=[
            pltpu.VMEM((EXPERTS, CAP, WIDE), BF16),
            pltpu.VMEM((EXPERTS, WIDE, QH * HD), BF16),
            pltpu.SemaphoreType.DMA((2, EXPERTS)),
        ],
        cost_estimate=pl.CostEstimate(
            flops=2 * EXPERTS * CAP * WIDE * QH * HD,
            bytes_accessed=EXPERTS * WIDE * (CAP + QH * HD) * 2,
            transcendentals=0,
        ),
        compiler_params=params(50),
        name="queries",
    )(rows, weight)


def attend_kernel(masked, place_ref, own_ref, q_ref, pos_ref, kv_hbm, out_ref, kv_ref, top_ref, acc_ref, sems):
    z = place_ref[0]

    def wanted(i):
        return pl.when(i < z) if i < Z - 1 else pl.when(own_ref[0] > 0)

    loads = [
        pltpu.make_async_copy(kv_hbm.at[i if i < Z - 1 else z], kv_ref.at[i], sems.at[i])
        for i in range(Z)
    ]
    for i in range(Z):
        wanted(i)(lambda i=i: loads[i].start())
    top_ref[...] = jnp.full(top_ref.shape, NEG, F32)
    acc_ref[...] = jnp.zeros(acc_ref.shape, F32)

    def block(i):
        mask = masked and i == Z - 1
        loads[i].wait()
        k = kv_ref[i, :, :HD]
        v = jnp.concatenate([kv_ref[i, :, HD:], jnp.ones((TOK, HD), BF16)], axis=1)
        scores = [nt(q_ref[h], k) for h in range(QH)]
        for h in range(QH):
            s = scores[h]
            if mask:
                place = lax.broadcasted_iota(jnp.int32, (CAP, TOK), 1).astype(F32)
                s = jnp.where(place <= pos_ref[:, 0:1], s, NEG)
            old = top_ref[h]
            new = jnp.maximum(old, jnp.max(s, axis=1, keepdims=True))
            p = jnp.exp2((s - jnp.concatenate([new] * (TOK // 128), axis=1)) * SCALE2)
            shrink = jnp.exp2((old - new) * SCALE2)
            acc_ref[h] = acc_ref[h] * jnp.concatenate([shrink, shrink], axis=1) + jnp.dot(
                p.astype(BF16), v, preferred_element_type=F32
            )
            top_ref[h] = new

    for i in range(Z):
        wanted(i)(lambda i=i: block(i))

    for h in range(QH):
        total = acc_ref[h, :, HD:]
        some = total > 0.0
        safe = jnp.where(some, total, 1.0)
        out_ref[h, :CAP, :] = (acc_ref[h, :, :HD] / safe).astype(BF16)
        out_ref[h, CAP:STAT, :] = jnp.zeros((STAT - CAP, HD), BF16)
        stat = jnp.where(some, top_ref[h] * SCALE2 + jnp.log2(safe), NEG)
        stat = jnp.concatenate([stat, jnp.zeros((256 - CAP, HD), F32)], axis=0).T[0:16, :]
        line = lax.broadcasted_iota(jnp.int32, (16, HD), 0)
        spread = jnp.where(lax.rem(line, 2) == 0, stat[:, :HD], stat[:, HD:])
        high = spread.astype(BF16).astype(F32)
        middle = (spread - high).astype(BF16).astype(F32)
        low = spread - high - middle
        parts = jnp.where(line < 2, high, jnp.where(line < 4, middle, low))
        out_ref[h, STAT:, :] = parts.astype(BF16)


def attend(masked, place, own, q, pos, blocks):
    name = "attend_own" if masked else "attend_near"
    return pl.pallas_call(
        lambda *refs: attend_kernel(masked, *refs),
        in_specs=[pl.BlockSpec(memory_space=pltpu.SMEM)] * 2
        + [pl.BlockSpec(memory_space=pltpu.VMEM)] * 2
        + [pl.BlockSpec(memory_space=pl.ANY)],
        out_specs=pl.BlockSpec(memory_space=pltpu.VMEM),
        out_shape=jax.ShapeDtypeStruct((QH, STAT + 16, HD), BF16),
        scratch_shapes=[
            pltpu.VMEM((Z, TOK, 2 * HD), BF16),
            pltpu.VMEM((QH, CAP, HD), F32),
            pltpu.VMEM((QH, CAP, 2 * HD), F32),
            pltpu.SemaphoreType.DMA((Z,)),
        ],
        cost_estimate=pl.CostEstimate(
            flops=4 * QH * CAP * HD * 4 * TOK,
            bytes_accessed=8 * TOK * 2 * HD * 2,
            transcendentals=QH * CAP * 4 * TOK,
        ),
        compiler_params=params(),
        name=name,
    )(place, own, q, pos, blocks)


def combine_kernel(*refs):
    outs, out_ref = refs[:4], refs[4]
    for h in range(QH):
        logs = []
        for o in outs:
            parts = o[h, STAT:, :].astype(F32)
            even = parts[0:1] + parts[2:3] + parts[4:5]
            odd = parts[1:2] + parts[3:4] + parts[5:6]
            stat = jnp.concatenate([even, odd], axis=1)
            logs.append(jnp.broadcast_to(stat, (HD, 256)).T[:CAP, :])
        top = jnp.maximum(jnp.maximum(logs[0], logs[1]), jnp.maximum(logs[2], logs[3]))
        weights = [jnp.exp2(v - top) for v in logs]
        total = weights[0] + weights[1] + weights[2] + weights[3]
        summed = sum(w * o[h, :CAP, :].astype(F32) for w, o in zip(weights, outs))
        out_ref[:, h * HD : (h + 1) * HD] = (summed / total).astype(BF16)


def combine(outs):
    return pl.pallas_call(
        combine_kernel,
        out_shape=jax.ShapeDtypeStruct((CAP, QH * HD), BF16),
        compiler_params=params(),
        name="combine",
    )(*outs)


def output_kernel(
    place_ref, mine_ref, other_ref, w_hbm, slot_ref, gate_ref, out_ref, w_ref, acc_ref, sems
):
    x, y, core = place_ref[1], place_ref[2], place_ref[3]
    order = [
        lax.rem(y + (Y - j // 2), Y) * CORE + (core if j % 2 == 0 else 1 - core)
        for j in range(EXPERTS)
    ]
    held = [lax.rem(e + y * CORE + core, Z) for e in order]
    sides = [x] + [lax.rem(x + (X - s), X) for s in SHIFTS]
    loads = [
        [
            pltpu.make_async_copy(
                w_hbm.at[held[j], i],
                w_ref.at[j, pl.ds(pl.multiple_of(sides[i] * COLS, COLS), COLS), :],
                sems.at[j, i],
            )
            for i in range(X)
        ]
        for j in range(EXPERTS)
    ]
    for group in loads:
        for load in group:
            load.start()
    lane = lax.broadcasted_iota(jnp.int32, (TOK, HD), 1)
    for j in range(EXPERTS):
        rows = (mine_ref if j % 2 == 0 else other_ref)[j // 2]
        here = lane == order[j]
        slot = jnp.sum(jnp.where(here, slot_ref[...], 0.0), axis=1, keepdims=True).astype(jnp.int32)
        gate = jnp.sum(jnp.where(here, gate_ref[...], 0.0), axis=1, keepdims=True)
        hit = lax.broadcasted_iota(jnp.int32, (TOK, CAP), 1) == slot
        spread = jnp.where(hit, gate, 0.0).astype(BF16)
        for load in loads[j]:
            load.wait()
        projected = nt(rows, w_ref[j]).astype(BF16)
        part = jnp.dot(spread, projected, preferred_element_type=F32)
        if j == 0:
            acc_ref[...] = part
        elif j < EXPERTS - 1:
            acc_ref[...] += part
        else:
            out_ref[...] = (acc_ref[...] + part).astype(BF16)


def project_output(place, mine, other, weight, slots, gates):
    vmem = pl.BlockSpec(memory_space=pltpu.VMEM)
    return pl.pallas_call(
        output_kernel,
        in_specs=[
            pl.BlockSpec(memory_space=pltpu.SMEM),
            vmem,
            vmem,
            pl.BlockSpec(memory_space=pltpu.HBM),
            vmem,
            vmem,
        ],
        out_specs=vmem,
        out_shape=jax.ShapeDtypeStruct((TOK, WIDE), BF16),
        scratch_shapes=[
            pltpu.VMEM((EXPERTS, WIDE, QH * HD), BF16),
            pltpu.VMEM((TOK, WIDE), F32),
            pltpu.SemaphoreType.DMA((EXPERTS, X)),
        ],
        cost_estimate=pl.CostEstimate(
            flops=2 * EXPERTS * CAP * WIDE * (QH * HD + TOK),
            bytes_accessed=EXPERTS * WIDE * QH * HD * 2,
            transcendentals=0,
        ),
        compiler_params=params(48),
        name="output",
    )(place, mine, other, weight, slots, gates)


def turn(n, by):
    return [(i, (i + by) % n) for i in range(n)]


def local(tokens, keys, values, expert_ids, router_logits, query_weight, output_weight):
    z = lax.axis_index("z")
    x = lax.axis_index("x")
    y = lax.axis_index("y")
    core = lax.axis_index("core")
    me = y * CORE + core
    place = jnp.stack([z, x, y, core]).astype(jnp.int32)

    blocks = lax.all_gather(join(keys, values), "z", axis=0)

    piece = lax.ppermute(
        output_weight[0].T,
        CTX + EXP,
        [
            ((i * X + j) * EXPERTS + e, ((i + e) % Z * X + j) * EXPERTS + i)
            for i in range(Z)
            for j in range(X)
            for e in range(EXPERTS)
        ],
    )
    outgoing = dispatch(expert_ids.T, tokens)
    outgoing, piece = lax.optimization_barrier((outgoing, piece))
    pieces = [piece] + [lax.ppermute(piece, "x", turn(X, s)) for s in SHIFTS]
    prepared = prepare(me[None].astype(jnp.int32), expert_ids, router_logits)
    incoming = lax.all_to_all(outgoing, EXP, split_axis=0, concat_axis=0, tiled=True)
    incoming, (pos, slots, gates), place = lax.optimization_barrier((incoming, prepared, place))
    pieces, _ = lax.optimization_barrier((jnp.stack(pieces), incoming))
    columns = lax.all_gather(pieces, "z", axis=0)
    q = project_queries(incoming, query_weight)

    outs = []
    for s in SHIFTS:
        other = lax.ppermute(q, "x", turn(X, s))
        source = lax.rem(x + (X - s), X)
        outs.append(attend(False, place, (x < source)[None].astype(jnp.int32), other, pos, blocks))
    q, *outs = lax.optimization_barrier((q, *outs))
    returned = [lax.ppermute(o, "x", turn(X, X - s)) for s, o in zip(SHIFTS, outs)]
    own = attend(True, place, jnp.ones((1,), jnp.int32), q, pos, blocks)
    outs = [own] + returned
    attended = combine(outs)

    near = [lax.ppermute(attended, "y", turn(Y, s)) for s in range(1, Y)]
    mine = jnp.stack([attended] + near)
    other = lax.ppermute(mine, "core", [(0, 1), (1, 0)])
    return project_output(place, mine, other, columns, slots, gates)


def solution(mesh):
    fine = Mesh(mesh.devices.reshape(Z, X, Y, CORE), ("z", "x", "y", "core"))
    return jax.shard_map(
        local,
        mesh=fine,
        in_specs=(
            P(CTX, EXP),
            P(CTX, EXP),
            P(CTX, EXP),
            P(CTX, None),
            P(CTX, None),
            P(EXP, None, None),
            P(EXP, None, CTX),
        ),
        out_specs=P(CTX, EXP),
        check_vma=False,
    )
```

```python
import jax
import jax.numpy as jnp
from jax import lax
from jax.experimental import pallas as pl
from jax.experimental.pallas import tpu as pltpu
from jax.sharding import Mesh, PartitionSpec as P

QH = 4
HD = 128
Z, X, Y, CORE = 8, 4, 4, 2
EXPERTS = 8
TOK = 768
CAP = 216
STAT = 224
WIDE = 768
COLS = 192
SHIFTS = (1, 3, 2)
NEG = -1e30
SCALE2 = HD ** (-0.5) * 1.4426950408889634
F32 = jnp.float32
BF16 = jnp.bfloat16
CTX = ("z", "x")
EXP = ("y", "core")


def params(mebibytes=16):
    return pltpu.CompilerParams(vmem_limit_bytes=mebibytes * 1024 * 1024)


def whole(shape):
    return pl.BlockSpec(shape, lambda *_: (0,) * len(shape))


def nt(a, b):
    return lax.dot_general(a, b, (((1,), (1,)), ((), ())), preferred_element_type=F32)


def join_kernel(key_ref, value_ref, out_ref):
    out_ref[:, :HD] = key_ref[...]
    out_ref[:, HD:] = value_ref[...]


def join(keys, values):
    return pl.pallas_call(
        join_kernel,
        out_shape=jax.ShapeDtypeStruct((TOK, 2 * HD), BF16),
        compiler_params=params(60),
        name="join",
    )(keys, values)


def dispatch_kernel(
    ids_ref, tok_hbm, out_hbm, tok_ref, row_ref, load_sem, out_sems
):
    load = pltpu.make_async_copy(tok_hbm, tok_ref, load_sem)
    load.start()
    row = lax.broadcasted_iota(jnp.int32, (EXPERTS, TOK), 0)
    member = (ids_ref[0:1, :] == row) | (ids_ref[1:2, :] == row)
    before = lax.broadcasted_iota(jnp.int32, (TOK, TOK), 0) < lax.broadcasted_iota(
        jnp.int32, (TOK, TOK), 1
    )
    slots = jnp.dot(
        jnp.where(member, 1.0, 0.0).astype(BF16),
        jnp.where(before, 1.0, 0.0).astype(BF16),
        preferred_element_type=F32,
    )
    slots = jnp.where(member, slots, -1.0).astype(jnp.int32)
    load.wait()
    sends = []
    for e in range(EXPERTS):
        hit = lax.broadcasted_iota(jnp.int32, (CAP, TOK), 0) == slots[e : e + 1, :]
        row_ref[e] = jnp.dot(
            jnp.where(hit, 1.0, 0.0).astype(BF16), tok_ref[...], preferred_element_type=F32
        ).astype(BF16)
        send = pltpu.make_async_copy(row_ref.at[e], out_hbm.at[e], out_sems.at[e])
        send.start()
        sends.append(send)
    for send in sends:
        send.wait()


def dispatch(ids_t, tokens):
    return pl.pallas_call(
        dispatch_kernel,
        in_specs=[
            pl.BlockSpec(memory_space=pltpu.VMEM),
            pl.BlockSpec(memory_space=pltpu.HBM),
        ],
        out_specs=pl.BlockSpec(memory_space=pltpu.HBM),
        out_shape=jax.ShapeDtypeStruct((EXPERTS, CAP, WIDE), BF16),
        scratch_shapes=[
            pltpu.VMEM((TOK, WIDE), BF16),
            pltpu.VMEM((EXPERTS, CAP, WIDE), BF16),
            pltpu.SemaphoreType.DMA,
            pltpu.SemaphoreType.DMA((EXPERTS,)),
        ],
        cost_estimate=pl.CostEstimate(
            flops=2 * EXPERTS * CAP * TOK * WIDE,
            bytes_accessed=(EXPERTS * CAP + TOK) * WIDE * 2,
            transcendentals=0,
        ),
        compiler_params=params(60),
        name="dispatch",
    )(ids_t, tokens)


def prepare_kernel(me_ref, ids_ref, logit_ref, pos_ref, slot_ref, gate_ref):
    lane = lax.broadcasted_iota(jnp.int32, (TOK, HD), 1)
    first = ids_ref[:, 0:1] == lane
    second = ids_ref[:, 1:2] == lane
    member = first | second
    before = lax.broadcasted_iota(jnp.int32, (TOK, TOK), 1) < lax.broadcasted_iota(
        jnp.int32, (TOK, TOK), 0
    )
    slots = jnp.dot(
        jnp.where(before, 1.0, 0.0).astype(BF16),
        jnp.where(member, 1.0, 0.0).astype(BF16),
        preferred_element_type=F32,
    )
    slots = jnp.where(member, slots, -1.0)
    slot_ref[...] = slots
    l0, l1 = logit_ref[:, 0:1], logit_ref[:, 1:2]
    top = jnp.maximum(l0, l1)
    w0, w1 = jnp.exp(l0 - top), jnp.exp(l1 - top)
    total = w0 + w1
    gate_ref[...] = jnp.where(first, w0 / total, jnp.where(second, w1 / total, 0.0))
    mine = jnp.sum(jnp.where(lane == me_ref[0], slots, 0.0), axis=1, keepdims=True)
    hit = lax.broadcasted_iota(jnp.int32, (TOK, 256), 1) == mine.astype(jnp.int32)
    place = lax.broadcasted_iota(jnp.int32, (TOK, 256), 0).astype(F32)
    pos = jnp.max(jnp.where(hit, place, -1.0), axis=0, keepdims=True)
    pos = jnp.where(pos < 0.0, float(TOK - 1), pos)
    pos_ref[...] = jnp.broadcast_to(pos, (HD, 256)).T[:CAP, :]


def prepare(me, ids, logits):
    vmem = pl.BlockSpec(memory_space=pltpu.VMEM)
    return pl.pallas_call(
        prepare_kernel,
        in_specs=[pl.BlockSpec(memory_space=pltpu.SMEM), vmem, vmem],
        out_specs=[vmem] * 3,
        out_shape=[
            jax.ShapeDtypeStruct((CAP, HD), F32),
            jax.ShapeDtypeStruct((TOK, HD), F32),
            jax.ShapeDtypeStruct((TOK, HD), F32),
        ],
        compiler_params=params(),
        name="prepare",
    )(me, ids, logits)


def query_kernel(x_hbm, w_hbm, q_ref, x_ref, w_ref, sems):
    loads = []
    for j in range(EXPERTS):
        rows = pltpu.make_async_copy(x_hbm.at[j], x_ref.at[j], sems.at[0, j])
        weight = pltpu.make_async_copy(
            w_hbm.at[0, pl.ds(j * WIDE, WIDE), :], w_ref.at[j], sems.at[1, j]
        )
        rows.start()
        weight.start()
        loads.append((rows, weight))
    total = None
    for j, (rows, weight) in enumerate(loads):
        rows.wait()
        weight.wait()
        part = jnp.dot(x_ref[j], w_ref[j], preferred_element_type=F32)
        total = part if total is None else total + part
    for h in range(QH):
        q_ref[h] = total[:, h * HD : (h + 1) * HD].astype(BF16)


def project_queries(rows, weight):
    return pl.pallas_call(
        query_kernel,
        in_specs=[
            pl.BlockSpec(memory_space=pl.ANY),
            pl.BlockSpec(memory_space=pltpu.HBM),
        ],
        out_specs=pl.BlockSpec(memory_space=pltpu.VMEM),
        out_shape=jax.ShapeDtypeStruct((QH, CAP, HD), BF16),
        scratch_shapes=[
            pltpu.VMEM((EXPERTS, CAP, WIDE), BF16),
            pltpu.VMEM((EXPERTS, WIDE, QH * HD), BF16),
            pltpu.SemaphoreType.DMA((2, EXPERTS)),
        ],
        cost_estimate=pl.CostEstimate(
            flops=2 * EXPERTS * CAP * WIDE * QH * HD,
            bytes_accessed=EXPERTS * WIDE * (CAP + QH * HD) * 2,
            transcendentals=0,
        ),
        compiler_params=params(50),
        name="queries",
    )(rows, weight)


def attend_kernel(masked, place_ref, own_ref, q_ref, pos_ref, kv_hbm, out_ref, kv_ref, top_ref, acc_ref, sems):
    z = place_ref[0]

    def wanted(i):
        return pl.when(i < z) if i < Z - 1 else pl.when(own_ref[0] > 0)

    loads = [
        pltpu.make_async_copy(kv_hbm.at[i if i < Z - 1 else z], kv_ref.at[i], sems.at[i])
        for i in range(Z)
    ]
    for i in range(Z):
        wanted(i)(lambda i=i: loads[i].start())
    top_ref[...] = jnp.full(top_ref.shape, NEG, F32)
    acc_ref[...] = jnp.zeros(acc_ref.shape, F32)

    def block(i):
        mask = masked and i == Z - 1
        loads[i].wait()
        k = kv_ref[i, :, :HD]
        v = jnp.concatenate([kv_ref[i, :, HD:], jnp.ones((TOK, HD), BF16)], axis=1)
        scores = [nt(q_ref[h], k) for h in range(QH)]
        for h in range(QH):
            s = scores[h]
            if mask:
                place = lax.broadcasted_iota(jnp.int32, (CAP, TOK), 1).astype(F32)
                s = jnp.where(place <= pos_ref[:, 0:1], s, NEG)
            old = top_ref[h]
            new = jnp.maximum(old, jnp.max(s, axis=1, keepdims=True))
            p = jnp.exp2((s - jnp.concatenate([new] * (TOK // 128), axis=1)) * SCALE2)
            shrink = jnp.exp2((old - new) * SCALE2)
            acc_ref[h] = acc_ref[h] * jnp.concatenate([shrink, shrink], axis=1) + jnp.dot(
                p.astype(BF16), v, preferred_element_type=F32
            )
            top_ref[h] = new

    for i in range(Z):
        wanted(i)(lambda i=i: block(i))

    for h in range(QH):
        total = acc_ref[h, :, HD:]
        some = total > 0.0
        safe = jnp.where(some, total, 1.0)
        out_ref[h, :CAP, :] = (acc_ref[h, :, :HD] / safe).astype(BF16)
        out_ref[h, CAP:STAT, :] = jnp.zeros((STAT - CAP, HD), BF16)
        stat = jnp.where(some, top_ref[h] * SCALE2 + jnp.log2(safe), NEG)
        stat = jnp.concatenate([stat, jnp.zeros((256 - CAP, HD), F32)], axis=0).T[0:16, :]
        line = lax.broadcasted_iota(jnp.int32, (16, HD), 0)
        spread = jnp.where(lax.rem(line, 2) == 0, stat[:, :HD], stat[:, HD:])
        high = spread.astype(BF16).astype(F32)
        middle = (spread - high).astype(BF16).astype(F32)
        low = spread - high - middle
        parts = jnp.where(line < 2, high, jnp.where(line < 4, middle, low))
        out_ref[h, STAT:, :] = parts.astype(BF16)


def attend(masked, place, own, q, pos, blocks):
    name = "attend_own" if masked else "attend_near"
    return pl.pallas_call(
        lambda *refs: attend_kernel(masked, *refs),
        in_specs=[pl.BlockSpec(memory_space=pltpu.SMEM)] * 2
        + [pl.BlockSpec(memory_space=pltpu.VMEM)] * 2
        + [pl.BlockSpec(memory_space=pl.ANY)],
        out_specs=pl.BlockSpec(memory_space=pltpu.VMEM),
        out_shape=jax.ShapeDtypeStruct((QH, STAT + 16, HD), BF16),
        scratch_shapes=[
            pltpu.VMEM((Z, TOK, 2 * HD), BF16),
            pltpu.VMEM((QH, CAP, HD), F32),
            pltpu.VMEM((QH, CAP, 2 * HD), F32),
            pltpu.SemaphoreType.DMA((Z,)),
        ],
        cost_estimate=pl.CostEstimate(
            flops=4 * QH * CAP * HD * 4 * TOK,
            bytes_accessed=8 * TOK * 2 * HD * 2,
            transcendentals=QH * CAP * 4 * TOK,
        ),
        compiler_params=params(),
        name=name,
    )(place, own, q, pos, blocks)


def combine_kernel(*refs):
    outs, out_ref = refs[:4], refs[4]
    for h in range(QH):
        logs = []
        for o in outs:
            parts = o[h, STAT:, :].astype(F32)
            even = parts[0:1] + parts[2:3] + parts[4:5]
            odd = parts[1:2] + parts[3:4] + parts[5:6]
            stat = jnp.concatenate([even, odd], axis=1)
            logs.append(jnp.broadcast_to(stat, (HD, 256)).T[:CAP, :])
        top = jnp.maximum(jnp.maximum(logs[0], logs[1]), jnp.maximum(logs[2], logs[3]))
        weights = [jnp.exp2(v - top) for v in logs]
        total = weights[0] + weights[1] + weights[2] + weights[3]
        summed = sum(w * o[h, :CAP, :].astype(F32) for w, o in zip(weights, outs))
        out_ref[:, h * HD : (h + 1) * HD] = (summed / total).astype(BF16)


def combine(outs):
    return pl.pallas_call(
        combine_kernel,
        out_shape=jax.ShapeDtypeStruct((CAP, QH * HD), BF16),
        compiler_params=params(),
        name="combine",
    )(*outs)


def output_kernel(
    place_ref, mine_ref, other_ref, w_hbm, slot_ref, gate_ref, out_ref, w_ref, acc_ref, sems
):
    x, y, core = place_ref[1], place_ref[2], place_ref[3]
    order = [
        lax.rem(y + (Y - j // 2), Y) * CORE + (core if j % 2 == 0 else 1 - core)
        for j in range(EXPERTS)
    ]
    held = [lax.rem(e + y * CORE + core, Z) for e in order]
    sides = [x] + [lax.rem(x + (X - s), X) for s in SHIFTS]
    loads = [
        [
            pltpu.make_async_copy(
                w_hbm.at[held[j], i],
                w_ref.at[j, pl.ds(pl.multiple_of(sides[i] * COLS, COLS), COLS), :],
                sems.at[j, i],
            )
            for i in range(X)
        ]
        for j in range(EXPERTS)
    ]
    for group in loads:
        for load in group:
            load.start()
    lane = lax.broadcasted_iota(jnp.int32, (TOK, HD), 1)
    for j in range(EXPERTS):
        rows = (mine_ref if j % 2 == 0 else other_ref)[j // 2]
        here = lane == order[j]
        slot = jnp.sum(jnp.where(here, slot_ref[...], 0.0), axis=1, keepdims=True).astype(jnp.int32)
        gate = jnp.sum(jnp.where(here, gate_ref[...], 0.0), axis=1, keepdims=True)
        hit = lax.broadcasted_iota(jnp.int32, (TOK, CAP), 1) == slot
        spread = jnp.where(hit, gate, 0.0).astype(BF16)
        for load in loads[j]:
            load.wait()
        projected = nt(rows, w_ref[j]).astype(BF16)
        part = jnp.dot(spread, projected, preferred_element_type=F32)
        if j == 0:
            acc_ref[...] = part
        elif j < EXPERTS - 1:
            acc_ref[...] += part
        else:
            out_ref[...] = (acc_ref[...] + part).astype(BF16)


def project_output(place, mine, other, weight, slots, gates):
    vmem = pl.BlockSpec(memory_space=pltpu.VMEM)
    return pl.pallas_call(
        output_kernel,
        in_specs=[
            pl.BlockSpec(memory_space=pltpu.SMEM),
            vmem,
            vmem,
            pl.BlockSpec(memory_space=pltpu.HBM),
            vmem,
            vmem,
        ],
        out_specs=vmem,
        out_shape=jax.ShapeDtypeStruct((TOK, WIDE), BF16),
        scratch_shapes=[
            pltpu.VMEM((EXPERTS, WIDE, QH * HD), BF16),
            pltpu.VMEM((TOK, WIDE), F32),
            pltpu.SemaphoreType.DMA((EXPERTS, X)),
        ],
        cost_estimate=pl.CostEstimate(
            flops=2 * EXPERTS * CAP * WIDE * (QH * HD + TOK),
            bytes_accessed=EXPERTS * WIDE * QH * HD * 2,
            transcendentals=0,
        ),
        compiler_params=params(48),
        name="output",
    )(place, mine, other, weight, slots, gates)


def turn(n, by):
    return [(i, (i + by) % n) for i in range(n)]


def local(tokens, keys, values, expert_ids, router_logits, query_weight, output_weight):
    z = lax.axis_index("z")
    x = lax.axis_index("x")
    y = lax.axis_index("y")
    core = lax.axis_index("core")
    me = y * CORE + core
    place = jnp.stack([z, x, y, core]).astype(jnp.int32)

    piece = lax.ppermute(
        output_weight[0].T,
        CTX + EXP,
        [
            ((i * X + j) * EXPERTS + e, ((i + e) % Z * X + j) * EXPERTS + i)
            for i in range(Z)
            for j in range(X)
            for e in range(EXPERTS)
        ],
    )
    outgoing = dispatch(expert_ids.T, tokens)
    outgoing, joined, piece = lax.optimization_barrier((outgoing, join(keys, values), piece))

    blocks = lax.all_gather(joined, "z", axis=0)
    pieces = [piece] + [lax.ppermute(piece, "x", turn(X, s)) for s in SHIFTS]
    prepared = prepare(me[None].astype(jnp.int32), expert_ids, router_logits)
    incoming = lax.all_to_all(outgoing, EXP, split_axis=0, concat_axis=0, tiled=True)
    incoming, (pos, slots, gates), place = lax.optimization_barrier((incoming, prepared, place))
    pieces, _ = lax.optimization_barrier((jnp.stack(pieces), incoming))
    columns = lax.all_gather(pieces, "z", axis=0)
    q = project_queries(incoming, query_weight)

    outs = []
    for s in SHIFTS:
        other = lax.ppermute(q, "x", turn(X, s))
        source = lax.rem(x + (X - s), X)
        outs.append(attend(False, place, (x < source)[None].astype(jnp.int32), other, pos, blocks))
    q, *outs = lax.optimization_barrier((q, *outs))
    returned = [lax.ppermute(o, "x", turn(X, X - s)) for s, o in zip(SHIFTS, outs)]
    own = attend(True, place, jnp.ones((1,), jnp.int32), q, pos, blocks)
    outs = [own] + returned
    attended = combine(outs)

    near = [lax.ppermute(attended, "y", turn(Y, s)) for s in range(1, Y)]
    mine = jnp.stack([attended] + near)
    other = lax.ppermute(mine, "core", [(0, 1), (1, 0)])
    return project_output(place, mine, other, columns, slots, gates)


def solution(mesh):
    fine = Mesh(mesh.devices.reshape(Z, X, Y, CORE), ("z", "x", "y", "core"))
    return jax.shard_map(
        local,
        mesh=fine,
        in_specs=(
            P(CTX, EXP),
            P(CTX, EXP),
            P(CTX, EXP),
            P(CTX, None),
            P(CTX, None),
            P(EXP, None, None),
            P(EXP, None, CTX),
        ),
        out_specs=P(CTX, EXP),
        check_vma=False,
    )
```

```python
import jax
import jax.numpy as jnp
from jax import lax
from jax.experimental import pallas as pl
from jax.experimental.pallas import tpu as pltpu
from jax.sharding import Mesh, PartitionSpec as P

QH = 4
HD = 128
Z, X, Y, CORE = 8, 4, 4, 2
EXPERTS = 8
TOK = 768
CAP = 216
STAT = 224
WIDE = 768
COLS = 192
SHIFTS = (1, 3, 2)
NEG = -1e30
SCALE2 = HD ** (-0.5) * 1.4426950408889634
F32 = jnp.float32
BF16 = jnp.bfloat16
CTX = ("z", "x")
EXP = ("y", "core")


def params(mebibytes=16):
    return pltpu.CompilerParams(vmem_limit_bytes=mebibytes * 1024 * 1024)


def whole(shape):
    return pl.BlockSpec(shape, lambda *_: (0,) * len(shape))


def nt(a, b):
    return lax.dot_general(a, b, (((1,), (1,)), ((), ())), preferred_element_type=F32)


def join_kernel(key_ref, value_ref, out_ref):
    out_ref[:, :HD] = key_ref[...]
    out_ref[:, HD:] = value_ref[...]


def join(keys, values):
    return pl.pallas_call(
        join_kernel,
        out_shape=jax.ShapeDtypeStruct((TOK, 2 * HD), BF16),
        compiler_params=params(60),
        name="join",
    )(keys, values)


def dispatch_kernel(
    ids_ref, tok_hbm, out_hbm, tok_ref, row_ref, load_sem, out_sems
):
    load = pltpu.make_async_copy(tok_hbm, tok_ref, load_sem)
    load.start()
    row = lax.broadcasted_iota(jnp.int32, (EXPERTS, TOK), 0)
    member = (ids_ref[0:1, :] == row) | (ids_ref[1:2, :] == row)
    before = lax.broadcasted_iota(jnp.int32, (TOK, TOK), 0) < lax.broadcasted_iota(
        jnp.int32, (TOK, TOK), 1
    )
    slots = jnp.dot(
        jnp.where(member, 1.0, 0.0).astype(BF16),
        jnp.where(before, 1.0, 0.0).astype(BF16),
        preferred_element_type=F32,
    )
    slots = jnp.where(member, slots, -1.0).astype(jnp.int32)
    load.wait()
    sends = []
    for e in range(EXPERTS):
        hit = lax.broadcasted_iota(jnp.int32, (CAP, TOK), 0) == slots[e : e + 1, :]
        row_ref[e] = jnp.dot(
            jnp.where(hit, 1.0, 0.0).astype(BF16), tok_ref[...], preferred_element_type=F32
        ).astype(BF16)
        send = pltpu.make_async_copy(row_ref.at[e], out_hbm.at[e], out_sems.at[e])
        send.start()
        sends.append(send)
    for send in sends:
        send.wait()


def dispatch(ids_t, tokens):
    return pl.pallas_call(
        dispatch_kernel,
        in_specs=[
            pl.BlockSpec(memory_space=pltpu.VMEM),
            pl.BlockSpec(memory_space=pltpu.HBM),
        ],
        out_specs=pl.BlockSpec(memory_space=pltpu.HBM),
        out_shape=jax.ShapeDtypeStruct((EXPERTS, CAP, WIDE), BF16),
        scratch_shapes=[
            pltpu.VMEM((TOK, WIDE), BF16),
            pltpu.VMEM((EXPERTS, CAP, WIDE), BF16),
            pltpu.SemaphoreType.DMA,
            pltpu.SemaphoreType.DMA((EXPERTS,)),
        ],
        cost_estimate=pl.CostEstimate(
            flops=2 * EXPERTS * CAP * TOK * WIDE,
            bytes_accessed=(EXPERTS * CAP + TOK) * WIDE * 2,
            transcendentals=0,
        ),
        compiler_params=params(60),
        name="dispatch",
    )(ids_t, tokens)


def prepare_kernel(me_ref, ids_ref, logit_ref, pos_ref, slot_ref, gate_ref):
    lane = lax.broadcasted_iota(jnp.int32, (TOK, HD), 1)
    first = ids_ref[:, 0:1] == lane
    second = ids_ref[:, 1:2] == lane
    member = first | second
    before = lax.broadcasted_iota(jnp.int32, (TOK, TOK), 1) < lax.broadcasted_iota(
        jnp.int32, (TOK, TOK), 0
    )
    slots = jnp.dot(
        jnp.where(before, 1.0, 0.0).astype(BF16),
        jnp.where(member, 1.0, 0.0).astype(BF16),
        preferred_element_type=F32,
    )
    slots = jnp.where(member, slots, -1.0)
    slot_ref[...] = slots
    l0, l1 = logit_ref[:, 0:1], logit_ref[:, 1:2]
    top = jnp.maximum(l0, l1)
    w0, w1 = jnp.exp(l0 - top), jnp.exp(l1 - top)
    total = w0 + w1
    gate_ref[...] = jnp.where(first, w0 / total, jnp.where(second, w1 / total, 0.0))
    mine = jnp.sum(jnp.where(lane == me_ref[0], slots, 0.0), axis=1, keepdims=True)
    hit = lax.broadcasted_iota(jnp.int32, (TOK, 256), 1) == mine.astype(jnp.int32)
    place = lax.broadcasted_iota(jnp.int32, (TOK, 256), 0).astype(F32)
    pos = jnp.max(jnp.where(hit, place, -1.0), axis=0, keepdims=True)
    pos = jnp.where(pos < 0.0, float(TOK - 1), pos)
    pos_ref[...] = jnp.broadcast_to(pos, (HD, 256)).T[:CAP, :]


def prepare(me, ids, logits):
    vmem = pl.BlockSpec(memory_space=pltpu.VMEM)
    return pl.pallas_call(
        prepare_kernel,
        in_specs=[pl.BlockSpec(memory_space=pltpu.SMEM), vmem, vmem],
        out_specs=[vmem] * 3,
        out_shape=[
            jax.ShapeDtypeStruct((CAP, HD), F32),
            jax.ShapeDtypeStruct((TOK, HD), F32),
            jax.ShapeDtypeStruct((TOK, HD), F32),
        ],
        compiler_params=params(),
        name="prepare",
    )(me, ids, logits)


def query_kernel(x_hbm, w_hbm, q_ref, x_ref, w_ref, sems):
    loads = []
    for j in range(EXPERTS):
        rows = pltpu.make_async_copy(x_hbm.at[j], x_ref.at[j], sems.at[0, j])
        weight = pltpu.make_async_copy(
            w_hbm.at[0, pl.ds(j * WIDE, WIDE), :], w_ref.at[j], sems.at[1, j]
        )
        rows.start()
        weight.start()
        loads.append((rows, weight))
    total = None
    for j, (rows, weight) in enumerate(loads):
        rows.wait()
        weight.wait()
        part = jnp.dot(x_ref[j], w_ref[j], preferred_element_type=F32)
        total = part if total is None else total + part
    for h in range(QH):
        q_ref[h] = total[:, h * HD : (h + 1) * HD].astype(BF16)


def project_queries(rows, weight):
    return pl.pallas_call(
        query_kernel,
        in_specs=[
            pl.BlockSpec(memory_space=pl.ANY),
            pl.BlockSpec(memory_space=pltpu.HBM),
        ],
        out_specs=pl.BlockSpec(memory_space=pltpu.VMEM),
        out_shape=jax.ShapeDtypeStruct((QH, CAP, HD), BF16),
        scratch_shapes=[
            pltpu.VMEM((EXPERTS, CAP, WIDE), BF16),
            pltpu.VMEM((EXPERTS, WIDE, QH * HD), BF16),
            pltpu.SemaphoreType.DMA((2, EXPERTS)),
        ],
        cost_estimate=pl.CostEstimate(
            flops=2 * EXPERTS * CAP * WIDE * QH * HD,
            bytes_accessed=EXPERTS * WIDE * (CAP + QH * HD) * 2,
            transcendentals=0,
        ),
        compiler_params=params(50),
        name="queries",
    )(rows, weight)


def attend_kernel(masked, place_ref, own_ref, q_ref, pos_ref, kv_hbm, out_ref, kv_ref, top_ref, acc_ref, sems):
    z = place_ref[0]

    def wanted(i):
        return pl.when(i < z) if i < Z - 1 else pl.when(own_ref[0] > 0)

    loads = [
        pltpu.make_async_copy(kv_hbm.at[i if i < Z - 1 else z], kv_ref.at[i], sems.at[i])
        for i in range(Z)
    ]
    for i in range(Z):
        wanted(i)(lambda i=i: loads[i].start())
    top_ref[...] = jnp.full(top_ref.shape, NEG, F32)
    acc_ref[...] = jnp.zeros(acc_ref.shape, F32)

    def block(i):
        mask = masked and i == Z - 1
        loads[i].wait()
        k = kv_ref[i, :, :HD]
        v = jnp.concatenate([kv_ref[i, :, HD:], jnp.ones((TOK, HD), BF16)], axis=1)
        scores = [nt(q_ref[h], k) for h in range(QH)]
        for h in range(QH):
            s = scores[h]
            if mask:
                place = lax.broadcasted_iota(jnp.int32, (CAP, TOK), 1).astype(F32)
                s = jnp.where(place <= pos_ref[:, 0:1], s, NEG)
            old = top_ref[h]
            new = jnp.maximum(old, jnp.max(s, axis=1, keepdims=True))
            p = jnp.exp2((s - jnp.concatenate([new] * (TOK // 128), axis=1)) * SCALE2)
            shrink = jnp.exp2((old - new) * SCALE2)
            acc_ref[h] = acc_ref[h] * jnp.concatenate([shrink, shrink], axis=1) + jnp.dot(
                p.astype(BF16), v, preferred_element_type=F32
            )
            top_ref[h] = new

    for i in range(Z):
        wanted(i)(lambda i=i: block(i))

    for h in range(QH):
        total = acc_ref[h, :, HD:]
        some = total > 0.0
        safe = jnp.where(some, total, 1.0)
        out_ref[h, :CAP, :] = (acc_ref[h, :, :HD] / safe).astype(BF16)
        out_ref[h, CAP:STAT, :] = jnp.zeros((STAT - CAP, HD), BF16)
        stat = jnp.where(some, top_ref[h] * SCALE2 + jnp.log2(safe), NEG)
        stat = jnp.concatenate([stat, jnp.zeros((256 - CAP, HD), F32)], axis=0).T[0:16, :]
        line = lax.broadcasted_iota(jnp.int32, (16, HD), 0)
        spread = jnp.where(lax.rem(line, 2) == 0, stat[:, :HD], stat[:, HD:])
        high = spread.astype(BF16).astype(F32)
        middle = (spread - high).astype(BF16).astype(F32)
        low = spread - high - middle
        parts = jnp.where(line < 2, high, jnp.where(line < 4, middle, low))
        out_ref[h, STAT:, :] = parts.astype(BF16)


def attend(masked, place, own, q, pos, blocks):
    name = "attend_own" if masked else "attend_near"
    return pl.pallas_call(
        lambda *refs: attend_kernel(masked, *refs),
        in_specs=[pl.BlockSpec(memory_space=pltpu.SMEM)] * 2
        + [pl.BlockSpec(memory_space=pltpu.VMEM)] * 2
        + [pl.BlockSpec(memory_space=pl.ANY)],
        out_specs=pl.BlockSpec(memory_space=pltpu.VMEM),
        out_shape=jax.ShapeDtypeStruct((QH, STAT + 16, HD), BF16),
        scratch_shapes=[
            pltpu.VMEM((Z, TOK, 2 * HD), BF16),
            pltpu.VMEM((QH, CAP, HD), F32),
            pltpu.VMEM((QH, CAP, 2 * HD), F32),
            pltpu.SemaphoreType.DMA((Z,)),
        ],
        cost_estimate=pl.CostEstimate(
            flops=4 * QH * CAP * HD * 4 * TOK,
            bytes_accessed=8 * TOK * 2 * HD * 2,
            transcendentals=QH * CAP * 4 * TOK,
        ),
        compiler_params=params(),
        name=name,
    )(place, own, q, pos, blocks)


def combine_kernel(*refs):
    outs, out_ref = refs[:4], refs[4]
    for h in range(QH):
        logs = []
        for o in outs:
            parts = o[h, STAT:, :].astype(F32)
            even = parts[0:1] + parts[2:3] + parts[4:5]
            odd = parts[1:2] + parts[3:4] + parts[5:6]
            stat = jnp.concatenate([even, odd], axis=1)
            logs.append(jnp.broadcast_to(stat, (HD, 256)).T[:CAP, :])
        top = jnp.maximum(jnp.maximum(logs[0], logs[1]), jnp.maximum(logs[2], logs[3]))
        weights = [jnp.exp2(v - top) for v in logs]
        total = weights[0] + weights[1] + weights[2] + weights[3]
        summed = sum(w * o[h, :CAP, :].astype(F32) for w, o in zip(weights, outs))
        out_ref[:, h * HD : (h + 1) * HD] = (summed / total).astype(BF16)


def combine(outs):
    return pl.pallas_call(
        combine_kernel,
        out_shape=jax.ShapeDtypeStruct((CAP, QH * HD), BF16),
        compiler_params=params(),
        name="combine",
    )(*outs)


def output_kernel(
    place_ref, mine_ref, other_ref, w_hbm, slot_ref, gate_ref, out_ref, w_ref, acc_ref, sems
):
    x, y, core = place_ref[1], place_ref[2], place_ref[3]
    order = [
        lax.rem(y + (Y - j // 2), Y) * CORE + (core if j % 2 == 0 else 1 - core)
        for j in range(EXPERTS)
    ]
    held = [lax.rem(e + y * CORE + core, Z) for e in order]
    sides = [x] + [lax.rem(x + (X - s), X) for s in SHIFTS]
    loads = [
        [
            pltpu.make_async_copy(
                w_hbm.at[held[j], i],
                w_ref.at[j, pl.ds(pl.multiple_of(sides[i] * COLS, COLS), COLS), :],
                sems.at[j, i],
            )
            for i in range(X)
        ]
        for j in range(EXPERTS)
    ]
    for group in loads:
        for load in group:
            load.start()
    lane = lax.broadcasted_iota(jnp.int32, (TOK, HD), 1)
    for j in range(EXPERTS):
        rows = (mine_ref if j % 2 == 0 else other_ref)[j // 2]
        here = lane == order[j]
        slot = jnp.sum(jnp.where(here, slot_ref[...], 0.0), axis=1, keepdims=True).astype(jnp.int32)
        gate = jnp.sum(jnp.where(here, gate_ref[...], 0.0), axis=1, keepdims=True)
        hit = lax.broadcasted_iota(jnp.int32, (TOK, CAP), 1) == slot
        spread = jnp.where(hit, gate, 0.0).astype(BF16)
        for load in loads[j]:
            load.wait()
        projected = nt(rows, w_ref[j]).astype(BF16)
        part = jnp.dot(spread, projected, preferred_element_type=F32)
        if j == 0:
            acc_ref[...] = part
        elif j < EXPERTS - 1:
            acc_ref[...] += part
        else:
            out_ref[...] = (acc_ref[...] + part).astype(BF16)


def project_output(place, mine, other, weight, slots, gates):
    vmem = pl.BlockSpec(memory_space=pltpu.VMEM)
    return pl.pallas_call(
        output_kernel,
        in_specs=[
            pl.BlockSpec(memory_space=pltpu.SMEM),
            vmem,
            vmem,
            pl.BlockSpec(memory_space=pltpu.HBM),
            vmem,
            vmem,
        ],
        out_specs=vmem,
        out_shape=jax.ShapeDtypeStruct((TOK, WIDE), BF16),
        scratch_shapes=[
            pltpu.VMEM((EXPERTS, WIDE, QH * HD), BF16),
            pltpu.VMEM((TOK, WIDE), F32),
            pltpu.SemaphoreType.DMA((EXPERTS, X)),
        ],
        cost_estimate=pl.CostEstimate(
            flops=2 * EXPERTS * CAP * WIDE * (QH * HD + TOK),
            bytes_accessed=EXPERTS * WIDE * QH * HD * 2,
            transcendentals=0,
        ),
        compiler_params=params(48),
        name="output",
    )(place, mine, other, weight, slots, gates)


def turn(n, by):
    return [(i, (i + by) % n) for i in range(n)]


def local(tokens, keys, values, expert_ids, router_logits, query_weight, output_weight):
    z = lax.axis_index("z")
    x = lax.axis_index("x")
    y = lax.axis_index("y")
    core = lax.axis_index("core")
    me = y * CORE + core
    place = jnp.stack([z, x, y, core]).astype(jnp.int32)

    blocks = lax.all_gather(join(keys, values), "z", axis=0)

    moves = [
        ((i * X + j) * EXPERTS + e, ((i + e) % Z * X + j) * EXPERTS + i)
        for i in range(Z)
        for j in range(X)
        for e in range(EXPERTS)
    ]
    piece = output_weight[0].T
    early = lax.ppermute(piece[: COLS // 2], CTX + EXP, moves)
    outgoing = dispatch(expert_ids.T, tokens)
    outgoing, early, late = lax.optimization_barrier((outgoing, early, piece[COLS // 2 :]))
    late = lax.ppermute(late, CTX + EXP, moves)
    piece = jnp.concatenate([early, late], axis=0)
    pieces = [piece] + [lax.ppermute(piece, "x", turn(X, s)) for s in SHIFTS]
    prepared = prepare(me[None].astype(jnp.int32), expert_ids, router_logits)
    incoming = lax.all_to_all(outgoing, EXP, split_axis=0, concat_axis=0, tiled=True)
    incoming, (pos, slots, gates), place = lax.optimization_barrier((incoming, prepared, place))
    pieces, _ = lax.optimization_barrier((jnp.stack(pieces), incoming))
    columns = lax.all_gather(pieces, "z", axis=0)
    q = project_queries(incoming, query_weight)

    outs = []
    for s in SHIFTS:
        other = lax.ppermute(q, "x", turn(X, s))
        source = lax.rem(x + (X - s), X)
        outs.append(attend(False, place, (x < source)[None].astype(jnp.int32), other, pos, blocks))
    q, *outs = lax.optimization_barrier((q, *outs))
    returned = [lax.ppermute(o, "x", turn(X, X - s)) for s, o in zip(SHIFTS, outs)]
    own = attend(True, place, jnp.ones((1,), jnp.int32), q, pos, blocks)
    outs = [own] + returned
    attended = combine(outs)

    near = [lax.ppermute(attended, "y", turn(Y, s)) for s in range(1, Y)]
    mine = jnp.stack([attended] + near)
    other = lax.ppermute(mine, "core", [(0, 1), (1, 0)])
    return project_output(place, mine, other, columns, slots, gates)


def solution(mesh):
    fine = Mesh(mesh.devices.reshape(Z, X, Y, CORE), ("z", "x", "y", "core"))
    return jax.shard_map(
        local,
        mesh=fine,
        in_specs=(
            P(CTX, EXP),
            P(CTX, EXP),
            P(CTX, EXP),
            P(CTX, None),
            P(CTX, None),
            P(EXP, None, None),
            P(EXP, None, CTX),
        ),
        out_specs=P(CTX, EXP),
        check_vma=False,
    )
```

```python
import jax
import jax.numpy as jnp
from jax import lax
from jax.experimental import pallas as pl
from jax.experimental.pallas import tpu as pltpu
from jax.sharding import Mesh, PartitionSpec as P

QH = 4
HD = 128
Z, X, Y, CORE = 8, 4, 4, 2
EXPERTS = 8
TOK = 768
CAP = 216
STAT = 224
WIDE = 768
COLS = 192
SHIFTS = (1, 3, 2)
NEG = -1e30
SCALE2 = HD ** (-0.5) * 1.4426950408889634
F32 = jnp.float32
BF16 = jnp.bfloat16
CTX = ("z", "x")
EXP = ("y", "core")


def params(mebibytes=16):
    return pltpu.CompilerParams(vmem_limit_bytes=mebibytes * 1024 * 1024)


def whole(shape):
    return pl.BlockSpec(shape, lambda *_: (0,) * len(shape))


def nt(a, b):
    return lax.dot_general(a, b, (((1,), (1,)), ((), ())), preferred_element_type=F32)


def join_kernel(key_ref, value_ref, out_ref):
    out_ref[:, :HD] = key_ref[...]
    out_ref[:, HD:] = value_ref[...]


def join(keys, values):
    return pl.pallas_call(
        join_kernel,
        out_shape=jax.ShapeDtypeStruct((TOK, 2 * HD), BF16),
        compiler_params=params(60),
        name="join",
    )(keys, values)


def dispatch_kernel(
    ids_ref, tok_hbm, out_hbm, tok_ref, row_ref, load_sem, out_sems
):
    load = pltpu.make_async_copy(tok_hbm, tok_ref, load_sem)
    load.start()
    row = lax.broadcasted_iota(jnp.int32, (EXPERTS, TOK), 0)
    member = (ids_ref[0:1, :] == row) | (ids_ref[1:2, :] == row)
    before = lax.broadcasted_iota(jnp.int32, (TOK, TOK), 0) < lax.broadcasted_iota(
        jnp.int32, (TOK, TOK), 1
    )
    slots = jnp.dot(
        jnp.where(member, 1.0, 0.0).astype(BF16),
        jnp.where(before, 1.0, 0.0).astype(BF16),
        preferred_element_type=F32,
    )
    slots = jnp.where(member, slots, -1.0).astype(jnp.int32)
    load.wait()
    sends = []
    for e in range(EXPERTS):
        hit = lax.broadcasted_iota(jnp.int32, (CAP, TOK), 0) == slots[e : e + 1, :]
        row_ref[e] = jnp.dot(
            jnp.where(hit, 1.0, 0.0).astype(BF16), tok_ref[...], preferred_element_type=F32
        ).astype(BF16)
        send = pltpu.make_async_copy(row_ref.at[e], out_hbm.at[e], out_sems.at[e])
        send.start()
        sends.append(send)
    for send in sends:
        send.wait()


def dispatch(ids_t, tokens):
    return pl.pallas_call(
        dispatch_kernel,
        in_specs=[
            pl.BlockSpec(memory_space=pltpu.VMEM),
            pl.BlockSpec(memory_space=pltpu.HBM),
        ],
        out_specs=pl.BlockSpec(memory_space=pltpu.HBM),
        out_shape=jax.ShapeDtypeStruct((EXPERTS, CAP, WIDE), BF16),
        scratch_shapes=[
            pltpu.VMEM((TOK, WIDE), BF16),
            pltpu.VMEM((EXPERTS, CAP, WIDE), BF16),
            pltpu.SemaphoreType.DMA,
            pltpu.SemaphoreType.DMA((EXPERTS,)),
        ],
        cost_estimate=pl.CostEstimate(
            flops=2 * EXPERTS * CAP * TOK * WIDE,
            bytes_accessed=(EXPERTS * CAP + TOK) * WIDE * 2,
            transcendentals=0,
        ),
        compiler_params=params(60),
        name="dispatch",
    )(ids_t, tokens)


def prepare_kernel(me_ref, ids_ref, logit_ref, pos_ref, slot_ref, gate_ref):
    lane = lax.broadcasted_iota(jnp.int32, (TOK, HD), 1)
    first = ids_ref[:, 0:1] == lane
    second = ids_ref[:, 1:2] == lane
    member = first | second
    before = lax.broadcasted_iota(jnp.int32, (TOK, TOK), 1) < lax.broadcasted_iota(
        jnp.int32, (TOK, TOK), 0
    )
    slots = jnp.dot(
        jnp.where(before, 1.0, 0.0).astype(BF16),
        jnp.where(member, 1.0, 0.0).astype(BF16),
        preferred_element_type=F32,
    )
    slots = jnp.where(member, slots, -1.0)
    slot_ref[...] = slots
    l0, l1 = logit_ref[:, 0:1], logit_ref[:, 1:2]
    top = jnp.maximum(l0, l1)
    w0, w1 = jnp.exp(l0 - top), jnp.exp(l1 - top)
    total = w0 + w1
    gate_ref[...] = jnp.where(first, w0 / total, jnp.where(second, w1 / total, 0.0))
    mine = jnp.sum(jnp.where(lane == me_ref[0], slots, 0.0), axis=1, keepdims=True)
    hit = lax.broadcasted_iota(jnp.int32, (TOK, 256), 1) == mine.astype(jnp.int32)
    place = lax.broadcasted_iota(jnp.int32, (TOK, 256), 0).astype(F32)
    pos = jnp.max(jnp.where(hit, place, -1.0), axis=0, keepdims=True)
    pos = jnp.where(pos < 0.0, float(TOK - 1), pos)
    pos_ref[...] = jnp.broadcast_to(pos, (HD, 256)).T[:CAP, :]


def prepare(me, ids, logits):
    vmem = pl.BlockSpec(memory_space=pltpu.VMEM)
    return pl.pallas_call(
        prepare_kernel,
        in_specs=[pl.BlockSpec(memory_space=pltpu.SMEM), vmem, vmem],
        out_specs=[vmem] * 3,
        out_shape=[
            jax.ShapeDtypeStruct((CAP, HD), F32),
            jax.ShapeDtypeStruct((TOK, HD), F32),
            jax.ShapeDtypeStruct((TOK, HD), F32),
        ],
        compiler_params=params(),
        name="prepare",
    )(me, ids, logits)


def query_kernel(x_hbm, w_hbm, q_ref, x_ref, w_ref, sems):
    loads = []
    for j in range(EXPERTS):
        rows = pltpu.make_async_copy(x_hbm.at[j], x_ref.at[j], sems.at[0, j])
        weight = pltpu.make_async_copy(
            w_hbm.at[0, pl.ds(j * WIDE, WIDE), :], w_ref.at[j], sems.at[1, j]
        )
        rows.start()
        weight.start()
        loads.append((rows, weight))
    total = None
    for j, (rows, weight) in enumerate(loads):
        rows.wait()
        weight.wait()
        part = jnp.dot(x_ref[j], w_ref[j], preferred_element_type=F32)
        total = part if total is None else total + part
    for h in range(QH):
        q_ref[h] = total[:, h * HD : (h + 1) * HD].astype(BF16)


def project_queries(rows, weight):
    return pl.pallas_call(
        query_kernel,
        in_specs=[
            pl.BlockSpec(memory_space=pl.ANY),
            pl.BlockSpec(memory_space=pltpu.HBM),
        ],
        out_specs=pl.BlockSpec(memory_space=pltpu.VMEM),
        out_shape=jax.ShapeDtypeStruct((QH, CAP, HD), BF16),
        scratch_shapes=[
            pltpu.VMEM((EXPERTS, CAP, WIDE), BF16),
            pltpu.VMEM((EXPERTS, WIDE, QH * HD), BF16),
            pltpu.SemaphoreType.DMA((2, EXPERTS)),
        ],
        cost_estimate=pl.CostEstimate(
            flops=2 * EXPERTS * CAP * WIDE * QH * HD,
            bytes_accessed=EXPERTS * WIDE * (CAP + QH * HD) * 2,
            transcendentals=0,
        ),
        compiler_params=params(50),
        name="queries",
    )(rows, weight)


def attend_kernel(masked, place_ref, own_ref, q_ref, pos_ref, kv_hbm, out_ref, kv_ref, top_ref, acc_ref, sems):
    z = place_ref[0]
    count = z + own_ref[0]
    loads = [
        pltpu.make_async_copy(kv_hbm.at[i], kv_ref.at[i], sems.at[i]) for i in range(Z)
    ]
    for i in range(Z):
        pl.when(i < count)(lambda i=i: loads[i].start())
    top_ref[...] = jnp.full(top_ref.shape, NEG, F32)
    acc_ref[...] = jnp.zeros(acc_ref.shape, F32)

    def blocks(first, number, mask):
        for i in range(first, first + number):
            loads[i].wait()
        keys = number * TOK
        k = jnp.concatenate([kv_ref[first + i, :, :HD] for i in range(number)], axis=0)
        v = jnp.concatenate([kv_ref[first + i, :, HD:] for i in range(number)], axis=0)
        v = jnp.concatenate([v, jnp.ones((keys, HD), BF16)], axis=1)
        scores = [nt(q_ref[h], k) for h in range(QH)]
        for h in range(QH):
            s = scores[h]
            if mask:
                place = lax.broadcasted_iota(jnp.int32, (CAP, keys), 1) - (number - 1) * TOK
                s = jnp.where(place.astype(F32) <= pos_ref[:, 0:1], s, NEG)
            old = top_ref[h]
            new = jnp.maximum(old, jnp.max(s, axis=1, keepdims=True))
            p = jnp.exp2((s - jnp.concatenate([new] * (keys // HD), axis=1)) * SCALE2)
            shrink = jnp.exp2((old - new) * SCALE2)
            acc_ref[h] = acc_ref[h] * jnp.concatenate([shrink, shrink], axis=1) + jnp.dot(
                p.astype(BF16), v, preferred_element_type=F32
            )
            top_ref[h] = new

    for i in range(0, Z, 2):
        if masked:
            pl.when(i + 1 < z)(lambda i=i: blocks(i, 2, False))
            pl.when(i + 1 == z)(lambda i=i: blocks(i, 2, True))
            pl.when(i == z)(lambda i=i: blocks(i, 1, True))
        else:
            pl.when(i + 1 < count)(lambda i=i: blocks(i, 2, False))
            pl.when(i + 1 == count)(lambda i=i: blocks(i, 1, False))

    for h in range(QH):
        total = acc_ref[h, :, HD:]
        some = total > 0.0
        safe = jnp.where(some, total, 1.0)
        out_ref[h, :CAP, :] = (acc_ref[h, :, :HD] / safe).astype(BF16)
        out_ref[h, CAP:STAT, :] = jnp.zeros((STAT - CAP, HD), BF16)
        stat = jnp.where(some, top_ref[h] * SCALE2 + jnp.log2(safe), NEG)
        stat = jnp.concatenate([stat, jnp.zeros((256 - CAP, HD), F32)], axis=0).T[0:16, :]
        line = lax.broadcasted_iota(jnp.int32, (16, HD), 0)
        spread = jnp.where(lax.rem(line, 2) == 0, stat[:, :HD], stat[:, HD:])
        high = spread.astype(BF16).astype(F32)
        middle = (spread - high).astype(BF16).astype(F32)
        low = spread - high - middle
        parts = jnp.where(line < 2, high, jnp.where(line < 4, middle, low))
        out_ref[h, STAT:, :] = parts.astype(BF16)


def attend(masked, place, own, q, pos, blocks):
    name = "attend_own" if masked else "attend_near"
    return pl.pallas_call(
        lambda *refs: attend_kernel(masked, *refs),
        in_specs=[pl.BlockSpec(memory_space=pltpu.SMEM)] * 2
        + [pl.BlockSpec(memory_space=pltpu.VMEM)] * 2
        + [pl.BlockSpec(memory_space=pl.ANY)],
        out_specs=pl.BlockSpec(memory_space=pltpu.VMEM),
        out_shape=jax.ShapeDtypeStruct((QH, STAT + 16, HD), BF16),
        scratch_shapes=[
            pltpu.VMEM((Z, TOK, 2 * HD), BF16),
            pltpu.VMEM((QH, CAP, HD), F32),
            pltpu.VMEM((QH, CAP, 2 * HD), F32),
            pltpu.SemaphoreType.DMA((Z,)),
        ],
        cost_estimate=pl.CostEstimate(
            flops=4 * QH * CAP * HD * 4 * TOK,
            bytes_accessed=8 * TOK * 2 * HD * 2,
            transcendentals=QH * CAP * 4 * TOK,
        ),
        compiler_params=params(32),
        name=name,
    )(place, own, q, pos, blocks)


def combine_kernel(*refs):
    outs, out_ref = refs[:4], refs[4]
    for h in range(QH):
        logs = []
        for o in outs:
            parts = o[h, STAT:, :].astype(F32)
            even = parts[0:1] + parts[2:3] + parts[4:5]
            odd = parts[1:2] + parts[3:4] + parts[5:6]
            stat = jnp.concatenate([even, odd], axis=1)
            logs.append(jnp.broadcast_to(stat, (HD, 256)).T[:CAP, :])
        top = jnp.maximum(jnp.maximum(logs[0], logs[1]), jnp.maximum(logs[2], logs[3]))
        weights = [jnp.exp2(v - top) for v in logs]
        total = weights[0] + weights[1] + weights[2] + weights[3]
        summed = sum(w * o[h, :CAP, :].astype(F32) for w, o in zip(weights, outs))
        out_ref[:, h * HD : (h + 1) * HD] = (summed / total).astype(BF16)


def combine(outs):
    return pl.pallas_call(
        combine_kernel,
        out_shape=jax.ShapeDtypeStruct((CAP, QH * HD), BF16),
        compiler_params=params(),
        name="combine",
    )(*outs)


def output_kernel(
    place_ref, mine_ref, other_ref, w_hbm, slot_ref, gate_ref, out_ref, w_ref, acc_ref, sems
):
    y, core = place_ref[2], place_ref[3]
    order = [
        lax.rem(y + (Y - j // 2), Y) * CORE + (core if j % 2 == 0 else 1 - core)
        for j in range(EXPERTS)
    ]
    held = [lax.rem(e + y * CORE + core, Z) for e in order]
    loads = [
        [
            pltpu.make_async_copy(
                w_hbm.at[held[j], i],
                w_ref.at[j, pl.ds(i * COLS, COLS), :],
                sems.at[j, i],
            )
            for i in range(X)
        ]
        for j in range(EXPERTS)
    ]
    for group in loads:
        for load in group:
            load.start()
    lane = lax.broadcasted_iota(jnp.int32, (TOK, HD), 1)
    for j in range(EXPERTS):
        rows = (mine_ref if j % 2 == 0 else other_ref)[j // 2]
        here = lane == order[j]
        slot = jnp.sum(jnp.where(here, slot_ref[...], 0.0), axis=1, keepdims=True).astype(jnp.int32)
        gate = jnp.sum(jnp.where(here, gate_ref[...], 0.0), axis=1, keepdims=True)
        hit = lax.broadcasted_iota(jnp.int32, (TOK, CAP), 1) == slot
        spread = jnp.where(hit, gate, 0.0).astype(BF16)
        for load in loads[j]:
            load.wait()
        projected = nt(rows, w_ref[j]).astype(BF16)
        part = jnp.dot(spread, projected, preferred_element_type=F32)
        if j == 0:
            acc_ref[...] = part
        elif j < EXPERTS - 1:
            acc_ref[...] += part
        else:
            out_ref[...] = (acc_ref[...] + part).astype(BF16)


def project_output(place, mine, other, weight, slots, gates):
    vmem = pl.BlockSpec(memory_space=pltpu.VMEM)
    return pl.pallas_call(
        output_kernel,
        in_specs=[
            pl.BlockSpec(memory_space=pltpu.SMEM),
            vmem,
            vmem,
            pl.BlockSpec(memory_space=pltpu.HBM),
            vmem,
            vmem,
        ],
        out_specs=vmem,
        out_shape=jax.ShapeDtypeStruct((TOK, WIDE), BF16),
        scratch_shapes=[
            pltpu.VMEM((EXPERTS, WIDE, QH * HD), BF16),
            pltpu.VMEM((TOK, WIDE), F32),
            pltpu.SemaphoreType.DMA((EXPERTS, X)),
        ],
        cost_estimate=pl.CostEstimate(
            flops=2 * EXPERTS * CAP * WIDE * (QH * HD + TOK),
            bytes_accessed=EXPERTS * WIDE * QH * HD * 2,
            transcendentals=0,
        ),
        compiler_params=params(48),
        name="output",
    )(place, mine, other, weight, slots, gates)


def turn(n, by):
    return [(i, (i + by) % n) for i in range(n)]


def local(tokens, keys, values, expert_ids, router_logits, query_weight, output_weight):
    z = lax.axis_index("z")
    x = lax.axis_index("x")
    y = lax.axis_index("y")
    core = lax.axis_index("core")
    me = y * CORE + core
    place = jnp.stack([z, x, y, core]).astype(jnp.int32)

    blocks = lax.all_gather(join(keys, values), "z", axis=0)

    piece = lax.ppermute(
        output_weight[0].T,
        CTX + EXP,
        [
            ((i * X + j) * EXPERTS + e, ((i + e) % Z * X + j) * EXPERTS + i)
            for i in range(Z)
            for j in range(X)
            for e in range(EXPERTS)
        ],
    )
    outgoing = dispatch(expert_ids.T, tokens)
    outgoing, piece = lax.optimization_barrier((outgoing, piece))
    columns = lax.all_gather(piece, CTX, axis=0).reshape(Z, X, COLS, QH * HD)
    prepared = prepare(me[None].astype(jnp.int32), expert_ids, router_logits)
    incoming = lax.all_to_all(outgoing, EXP, split_axis=0, concat_axis=0, tiled=True)
    incoming, (pos, slots, gates), place = lax.optimization_barrier((incoming, prepared, place))
    q = project_queries(incoming, query_weight)

    outs = []
    for s in SHIFTS:
        other = lax.ppermute(q, "x", turn(X, s))
        source = lax.rem(x + (X - s), X)
        outs.append(attend(False, place, (x < source)[None].astype(jnp.int32), other, pos, blocks))
    q, *outs = lax.optimization_barrier((q, *outs))
    returned = [lax.ppermute(o, "x", turn(X, X - s)) for s, o in zip(SHIFTS, outs)]
    own = attend(True, place, jnp.ones((1,), jnp.int32), q, pos, blocks)
    outs = [own] + returned
    attended = combine(outs)

    near = [lax.ppermute(attended, "y", turn(Y, s)) for s in range(1, Y)]
    mine = jnp.stack([attended] + near)
    other = lax.ppermute(mine, "core", [(0, 1), (1, 0)])
    return project_output(place, mine, other, columns, slots, gates)


def solution(mesh):
    fine = Mesh(mesh.devices.reshape(Z, X, Y, CORE), ("z", "x", "y", "core"))
    return jax.shard_map(
        local,
        mesh=fine,
        in_specs=(
            P(CTX, EXP),
            P(CTX, EXP),
            P(CTX, EXP),
            P(CTX, None),
            P(CTX, None),
            P(EXP, None, None),
            P(EXP, None, CTX),
        ),
        out_specs=P(CTX, EXP),
        check_vma=False,
    )
```
